32 devices in a mesh: row: 4 (over y, x), col: 8 (over z, core).
Axes of the slice: x: 2, y: 2, z: 4, core: 2. Of those that a mesh axis runs over, the one named last changes fastest.
Arguments:
- vectors: float32 [16, 262144], P(None, ('row', 'col')), may hold values from -6 to 6
- coords: float32 [3, 262144], P(None, ('row', 'col')), may hold values from 0 to 1
- leaf_basis: bfloat16 [1024, 64, 256], P(('row', 'col')), may hold values from -0.375 to 0.375
- transfer: bfloat16 [2048, 4096], P(('row', 'col')), may hold values from -0.5 to 0.5
- coupling: bfloat16 [2048, 6, 4096], P(('row', 'col')), may hold values from -0.3125 to 0.3125
- near_list: int32 [1024, 8], P(('row', 'col')), may hold values from 0 to 1023, as said below
- near_count: int32 [1024], P(('row', 'col')), may hold values from 1 to 8, as said below
- local_list: int32 [2048, 6], P(('row', 'col')), may hold values from 1 to 2047, as said below
- top_transfer: bfloat16 [64, 4096], replicated, may hold values from -0.5 to 0.5
- top_coupling: bfloat16 [64, 2, 4096], replicated, may hold values from -0.5 to 0.5
- top_list: int32 [64, 2], replicated, may hold values from 1 to 63, as said below
Outputs:
- product: float32 [16, 262144], P(None, ('row', 'col'))
The draws below stay inside these ranges and needn't reach their ends.
Inputs may be any that keep to these rules, and one draw needn't show every extreme that they name: `near_list`: entry 0 of a leaf's list is the leaf itself; every entry names a leaf of the same device or of the device just before or after it in the order of row then col; entries past near_count are ignored. `near_count`: devices differ in how full their leaves' lists are. `local_list`: a slot's partners are slots of the same level of the subtrees of the same device or of the device just before or after it; the rows of slots 0 and 1 are ignored. `top_list`: a slot's partners are upper slots of the same level; rows 0 and 1 are ignored.
All inputs are finite; a program needn't handle non-finite values.
Results may differ from the reference program's by a relative error of at most 0.0003.
Values sent between devices are 32-bit elements; how exact they have to be, the bound alone decides.
A program may use at most 128 MiB of HBM per device.

```python
import math
import jax
import jax.numpy as jnp
from jax import lax

LEAF = 256
RANK = 64
VECS = 16
LEAF_DEV = 32
NEAR = 8
FAR = 6
TOP_FAR = 2
DEVS = 32
LEAVES = 1024
POINTS = 262144
SLOTS = 2048
TOP_SLOTS = 64
N_ROW = 4
N_COL = 8


def level_base(slot_ids, limit):
    safe = jnp.maximum(slot_ids, 1)
    level = jnp.zeros_like(safe)
    power = 1
    while power <= limit:
        level = level + (safe >= power).astype(jnp.int32)
        power = power * 2
    return jnp.power(2, level - 1).astype(jnp.int32)


def draw_near_list(key, part):
    leaf_ids = jnp.arange(LEAVES, dtype=jnp.int32)
    owner = leaf_ids // LEAF_DEV
    first_key, second_key = jax.random.split(jax.random.fold_in(key, 11))
    steps = jax.random.randint(first_key, (LEAVES, NEAR), -1, 2)
    partner_dev = jnp.clip(owner[:, None] + steps, 0, DEVS - 1)
    picks = jax.random.randint(second_key, (LEAVES, NEAR), 0, LEAF_DEV)
    chosen = partner_dev * LEAF_DEV + picks
    chosen = chosen.at[:, 0].set(leaf_ids)
    return chosen.astype(jnp.int32)


def draw_near_count(key, part):
    leaf_ids = jnp.arange(LEAVES, dtype=jnp.int32)
    owner = leaf_ids // LEAF_DEV
    first_key, second_key = jax.random.split(jax.random.fold_in(key, 23))
    ceiling = jax.random.randint(first_key, (DEVS,), 1, NEAR + 1)
    ceiling = ceiling.at[0].set(NEAR)
    spread = jax.random.randint(second_key, (LEAVES,), 0, NEAR)
    counts = 1 + spread % ceiling[owner]
    counts = counts.at[0].set(NEAR).at[1].set(1)
    return counts.astype(jnp.int32)


def draw_local_list(key, part):
    subtree = 2 * LEAF_DEV
    global_ids = jnp.arange(SLOTS, dtype=jnp.int32)
    owner = global_ids // subtree
    slot_ids = global_ids % subtree
    base = level_base(slot_ids, subtree)
    first_key, second_key = jax.random.split(jax.random.fold_in(key, 37))
    steps = jax.random.randint(first_key, (SLOTS, FAR), -1, 2)
    partner_dev = jnp.clip(owner[:, None] + steps, 0, DEVS - 1)
    picks = jax.random.randint(second_key, (SLOTS, FAR), 0, subtree) % base[:, None]
    chosen = partner_dev * subtree + base[:, None] + picks
    chosen = chosen.at[0, 0].set(1).at[SLOTS - 1, 0].set(SLOTS - 1)
    return chosen.astype(jnp.int32)


def draw_top_list(key, part):
    slot_ids = jnp.arange(TOP_SLOTS, dtype=jnp.int32)
    base = level_base(slot_ids, TOP_SLOTS)
    picks = jax.random.randint(jax.random.fold_in(key, 41), (TOP_SLOTS, TOP_FAR), 0, TOP_SLOTS) % base[:, None]
    chosen = base[:, None] + picks
    chosen = chosen.at[TOP_SLOTS - 1, 0].set(TOP_SLOTS - 1)
    return chosen.astype(jnp.int32)


def block_scale(rng, dims, cuts, smallest, top_value):
    loudness = 1.0
    for axis_at, parts in cuts:
        steps = jax.random.uniform(jax.random.fold_in(jax.random.fold_in(rng, 6), axis_at), (parts,), jnp.float32, smallest / len(cuts), top_value / len(cuts))
        loudness = loudness * jnp.repeat(jnp.exp(steps), dims[axis_at] // parts).reshape((-1,) + (1,) * (len(dims) - 1 - axis_at))
    return loudness


def scatter_about(rng, extent, scale, bound, shards=(), held_as=jnp.bfloat16):
    array = jax.random.normal(rng, extent, jnp.float32) * scale
    if len(shards) > 0:
        array = block_scale(rng, extent, shards, -0.22, 0.18) * array
    return jnp.clip(array, min=-bound, max=bound).astype(held_as)


def setup_inputs(seed: int = 0) -> dict:
    key_of = jax.random.split(jax.random.key(seed), 12)
    vectors = scatter_about(key_of[0], (VECS, POINTS), 1.0, 6.0, ((1, 32),), jnp.float32)
    coords = jnp.clip(1.0 * jax.random.uniform(key_of[1], (3, POINTS), jnp.float32) ** block_scale(key_of[1], (3, POINTS), ((1, 32),), -0.2, 0.2), 0.0, 1.0)
    leaf_basis = scatter_about(key_of[2], (LEAVES, RANK, LEAF), LEAF ** -0.5, 0.375, ((0, 32),))
    transfer = scatter_about(key_of[3], (SLOTS, RANK * RANK), (2 * RANK) ** -0.5, 0.5, ((0, 32),))
    coupling = scatter_about(key_of[4], (SLOTS, FAR, RANK * RANK), (FAR * RANK) ** -0.5, 0.3125, ((0, 32),))
    near_list = draw_near_list(jax.random.fold_in(key_of[11], 71), 0)
    near_count = draw_near_count(jax.random.fold_in(key_of[11], 71), 0)
    local_list = draw_local_list(jax.random.fold_in(key_of[11], 71), 0)
    top_transfer = scatter_about(key_of[8], (TOP_SLOTS, RANK * RANK), (2 * RANK) ** -0.5, 0.5)
    top_coupling = scatter_about(key_of[9], (TOP_SLOTS, TOP_FAR, RANK * RANK), (TOP_FAR * RANK) ** -0.5, 0.5)
    top_list = draw_top_list(jax.random.fold_in(key_of[11], 71), 0)
    return dict(vectors=vectors, coords=coords, leaf_basis=leaf_basis, transfer=transfer, coupling=coupling, near_list=near_list, near_count=near_count, local_list=local_list, top_transfer=top_transfer, top_coupling=top_coupling, top_list=top_list)


HIGHEST_PREC = lax.Precision.HIGHEST
ROOT_THREE = 1.7320508075688772
LENGTH_SCALE = 0.2
JITTER_SQ = 0.0001

def near_leaf(own_coords, partner_ids, partner_count, table):
    chosen = jnp.take(table, partner_ids, axis=1)
    offsets = own_coords[:, :, None, None] - chosen[:3, None, :, :]
    distance = jnp.sqrt(lax.optimization_barrier(jnp.sum(offsets * offsets, axis=0)) + JITTER_SQ)
    scaled = ROOT_THREE * distance / LENGTH_SCALE
    active = (jnp.arange(partner_ids.shape[0], dtype=jnp.int32) < partner_count).astype(jnp.float32)
    matern = (1.0 + scaled) * jnp.exp(-scaled) * active[None, :, None] / math.sqrt(own_coords.shape[1])
    return jnp.einsum('anb,vnb->va', matern, chosen[3:], precision=HIGHEST_PREC)

def upward_level(skeleton, matrices, half_size):
    children = skeleton[..., 2 * half_size:4 * half_size, :, :]
    blocks = matrices[..., 2 * half_size:4 * half_size, :, :]
    products = jnp.einsum('...svr,...srq->...svq', children, blocks, precision=HIGHEST_PREC)
    new_shape = products.shape[:-3] + (half_size, 2) + products.shape[-2:]
    return products.reshape(new_shape).sum(axis=-3)

def downward_level(field, matrices, half_size):
    parents = field[..., half_size:2 * half_size, :, :]
    doubled = jnp.repeat(parents, 2, axis=-3)
    blocks = matrices[..., 2 * half_size:4 * half_size, :, :]
    added = jnp.einsum('...svq,...srq->...svr', doubled, blocks, precision=HIGHEST_PREC)
    return field.at[..., 2 * half_size:4 * half_size, :, :].add(added)

def reference(vectors, coords, leaf_basis, transfer, coupling, near_list, near_count, local_list, top_transfer, top_coupling, top_list):
    devices = N_ROW * N_COL
    subtree = 2 * LEAF_DEV
    basis = leaf_basis.astype(jnp.float32)
    grouped = vectors.reshape(VECS, LEAVES, LEAF).transpose(1, 0, 2)
    leaf_skel = jnp.einsum('cvl,crl->cvr', grouped, basis, precision=HIGHEST_PREC)
    matrices = transfer.astype(jnp.float32).reshape(devices, subtree, RANK, RANK)
    skeleton = jnp.zeros((devices, subtree, VECS, RANK), jnp.float32)
    skeleton = skeleton.at[:, LEAF_DEV:].set(leaf_skel.reshape(devices, LEAF_DEV, VECS, RANK))
    half_size = LEAF_DEV // 2
    while half_size >= 1:
        skeleton = skeleton.at[:, half_size:2 * half_size].set(upward_level(skeleton, matrices, half_size))
        half_size = half_size // 2
    top_mats = top_transfer.astype(jnp.float32).reshape(2 * devices, RANK, RANK)
    upper = jnp.zeros((2 * devices, VECS, RANK), jnp.float32).at[devices:].set(skeleton[:, 1])
    half_size = devices // 2
    while half_size >= 2:
        upper = upper.at[half_size:2 * half_size].set(upward_level(upper, top_mats, half_size))
        half_size = half_size // 2
    top_blocks = top_coupling.astype(jnp.float32).reshape(2 * devices, TOP_FAR, RANK, RANK)
    upper_field = jnp.einsum('skvr,skrq->svq', upper[top_list], top_blocks, precision=HIGHEST_PREC)
    upper_field = upper_field.at[:2].set(0.0)
    half_size = 2
    while half_size < devices:
        upper_field = downward_level(upper_field, top_mats, half_size)
        half_size = half_size * 2
    flat = skeleton.reshape(devices * subtree, VECS, RANK)

    def couple_device(items):
        lists, blocks = items
        partners = flat[lists]
        mats = blocks.astype(jnp.float32).reshape(subtree, FAR, RANK, RANK)
        return jnp.einsum('skvr,skrq->svq', partners, mats, precision=HIGHEST_PREC)
    field = lax.map(couple_device, (local_list.reshape(devices, subtree, FAR), coupling.reshape(devices, subtree, FAR, RANK * RANK)))
    field = field.at[:, 0].set(0.0)
    field = field.at[:, 1].set(upper_field[devices:])
    half_size = 1
    while half_size < LEAF_DEV:
        field = downward_level(field, matrices, half_size)
        half_size = half_size * 2
    leaf_field = field[:, LEAF_DEV:].reshape(LEAVES, VECS, RANK)
    far_part = jnp.einsum('cvr,crl->cvl', leaf_field, basis, precision=HIGHEST_PREC)
    table = jnp.concatenate([coords, vectors], axis=0).reshape(3 + VECS, LEAVES, LEAF)
    own = coords.reshape(3, LEAVES, LEAF).transpose(1, 0, 2)

    def near_item(items):
        return near_leaf(items[0], items[1], items[2], table)
    near_part = lax.map(near_item, (own, near_list, near_count))
    return (far_part + near_part).transpose(1, 0, 2).reshape(VECS, POINTS)
```

```python
import math

import jax
import jax.numpy as jnp
from jax import lax
from jax.experimental import pallas as pl
from jax.experimental.pallas import tpu as pltpu
from jax.sharding import PartitionSpec as P

HIGHEST_PREC = lax.Precision.HIGHEST
ROOT_THREE = 1.7320508075688772
LENGTH_SCALE = 0.2
JITTER_SQ = 0.0001
LOG2E = 1.4426950408889634
AXES = ("row", "col")
UNROLL = 4
F32 = jnp.float32
BF16 = jnp.bfloat16


def pieces(value, count):
    parts = []
    for _ in range(count):
        part = value.astype(BF16).astype(F32)
        parts.append(part)
        value = value - part
    return parts


def near_kernel(
    leaf_dev,
    ids_ref,
    count_ref,
    vec_refs,
    xyz_refs,
    far_ref,
    out_ref,
    own_feat,
    pair_feat,
    pair_vecs,
    pair_list,
):
    vec_count, width = out_ref.shape
    leaf = width // leaf_dev
    me = lax.axis_index("row") * lax.axis_size("col") + lax.axis_index("col")
    offset = (me - 1) * leaf_dev
    gain = ROOT_THREE / LENGTH_SCALE * LOG2E
    jitter = JITTER_SQ * gain * gain
    vec_gain = 1.0 / (LOG2E * math.sqrt(leaf))

    def list_leaf(c, total):
        def add(m, t):
            pair_list[0, t] = c
            pair_list[1, t] = ids_ref[c, m] - offset
            return t + 1

        return lax.fori_loop(0, count_ref[c], add, total)

    total = lax.fori_loop(0, leaf_dev, list_leaf, 0)
    for i in range(UNROLL):
        pair_list[0, total + i] = 0
        pair_list[1, total + i] = 3 * leaf_dev
    pair_vecs[3 * leaf_dev] = jnp.zeros((2 * vec_count, leaf), BF16)

    row_ids = lax.broadcasted_iota(jnp.int32, (8, leaf), 0)

    def build(part, c):
        cols = pl.ds(pl.multiple_of(c * leaf, leaf), leaf)
        xyz = (xyz_refs[part][:, cols] - 0.5) * gain
        norm = jnp.sum(xyz * xyz, axis=0, keepdims=True)
        wide = jnp.concatenate([xyz, jnp.zeros((5, leaf), F32)], axis=0)
        theirs = jnp.where(row_ids == 3, norm, jnp.where(row_ids == 4, 1.0, wide))
        b1, b2, b3 = pieces(theirs, 3)
        slot = part * leaf_dev + c
        pair_feat[slot] = jnp.concatenate([b1, b2, b1, b2, b3, b1], axis=0).astype(BF16)
        hi, lo = pieces(vec_refs[part][:, cols] * vec_gain, 2)
        pair_vecs[slot] = jnp.concatenate([hi, lo], axis=0).astype(BF16)
        if part == 1:
            mine = jnp.where(
                row_ids == 4, norm + jitter, jnp.where(row_ids == 3, 1.0, -2.0 * wide)
            )
            a1, a2, a3 = pieces(mine, 3)
            stacked = jnp.concatenate([a1, a1, a2, a2, a1, a3], axis=0)
            own_feat[c] = jnp.transpose(stacked).astype(BF16)

    for part in range(3):
        pl.loop(0, leaf_dev)(lambda c, part=part: build(part, c))
    pair_feat[3 * leaf_dev] = pair_feat[leaf_dev]

    out_ref[...] = far_ref[...]

    def pair(t):
        c, p = pair_list[0, t], pair_list[1, t]
        square = jnp.dot(own_feat[c], pair_feat[p], preferred_element_type=F32)
        dist = square * lax.rsqrt(square)
        matern = (LOG2E + dist) * jnp.exp2(-dist)
        high = matern.astype(BF16)
        low = (matern - high.astype(F32)).astype(BF16)
        vecs = pair_vecs[p]
        dims = (((1,), (1,)), ((), ()))
        first = lax.dot_general(vecs, high, dims, preferred_element_type=F32)
        second = lax.dot_general(vecs[:vec_count], low, dims, preferred_element_type=F32)
        return c, first[:vec_count] + first[vec_count:] + second

    @pl.loop(0, (total + UNROLL - 1) // UNROLL)
    def _(step):
        done = [pair(step * UNROLL + i) for i in range(UNROLL)]
        for c, added in done:
            cols = pl.ds(pl.multiple_of(c * leaf, leaf), leaf)
            out_ref[:, cols] += added


def near_call(near_list, near_count, vecs, xyz, far):
    leaf_dev, near = near_list.shape
    vec_count, width = far.shape
    leaf = width // leaf_dev

    def body(ids, count, v0, v1, v2, c0, c1, c2, far_ref, out_ref, *scratch):
        near_kernel(
            leaf_dev, ids, count, (v0, v1, v2), (c0, c1, c2), far_ref, out_ref, *scratch
        )

    vmem = pl.BlockSpec(memory_space=pltpu.VMEM)
    smem = pl.BlockSpec(memory_space=pltpu.SMEM)
    return pl.pallas_call(
        body,
        out_shape=jax.ShapeDtypeStruct((vec_count, width), F32),
        in_specs=[smem, smem] + [vmem] * 7,
        out_specs=vmem,
        scratch_shapes=[
            pltpu.VMEM((leaf_dev, leaf, 48), BF16),
            pltpu.VMEM((3 * leaf_dev + 1, 48, leaf), BF16),
            pltpu.VMEM((3 * leaf_dev + 1, 2 * vec_count, leaf), BF16),
            pltpu.SMEM((2, leaf_dev * near + UNROLL), jnp.int32),
        ],
        compiler_params=pltpu.CompilerParams(vmem_limit_bytes=48 * 1024 * 1024),
        cost_estimate=pl.CostEstimate(
            flops=2 * leaf_dev * near * leaf * leaf * 64,
            bytes_accessed=7 * 4 * vec_count * width,
            transcendentals=2 * leaf_dev * near * leaf * leaf,
        ),
        name="near_pairs",
    )(near_list, near_count, *vecs, *xyz, far)


def upward_level(skeleton, matrices, half_size):
    children = skeleton[..., 2 * half_size : 4 * half_size, :, :]
    blocks = matrices[..., 2 * half_size : 4 * half_size, :, :]
    products = jnp.einsum("...svr,...srq->...svq", children, blocks, precision=HIGHEST_PREC)
    new_shape = products.shape[:-3] + (half_size, 2) + products.shape[-2:]
    return products.reshape(new_shape).sum(axis=-3)


def downward_level(field, matrices, half_size):
    parents = field[..., half_size : 2 * half_size, :, :]
    doubled = jnp.repeat(parents, 2, axis=-3)
    blocks = matrices[..., 2 * half_size : 4 * half_size, :, :]
    added = jnp.einsum("...svq,...srq->...svr", doubled, blocks, precision=HIGHEST_PREC)
    return field.at[..., 2 * half_size : 4 * half_size, :, :].add(added)


def per_device(
    vectors,
    coords,
    leaf_basis,
    transfer,
    coupling,
    near_list,
    near_count,
    local_list,
    top_transfer,
    top_coupling,
    top_list,
):
    leaf_dev = leaf_basis.shape[0]
    rank = leaf_basis.shape[1]
    leaf_size = leaf_basis.shape[2]
    vec_count = vectors.shape[0]
    far_count = coupling.shape[1]
    top_count = top_coupling.shape[1]
    subtree = 2 * leaf_dev
    devices = lax.axis_size(("row", "col"))
    position = lax.axis_index(("row", "col"))
    basis = leaf_basis.astype(jnp.float32)
    grouped = vectors.reshape(vec_count, leaf_dev, leaf_size)
    leaf_skel = jnp.einsum("vcl,crl->cvr", grouped, basis, precision=HIGHEST_PREC)
    matrices = transfer.astype(jnp.float32).reshape(subtree, rank, rank)
    skeleton = jnp.zeros((subtree, vec_count, rank), jnp.float32).at[leaf_dev:].set(leaf_skel)
    half_size = leaf_dev // 2
    while half_size >= 1:
        skeleton = skeleton.at[half_size : 2 * half_size].set(
            upward_level(skeleton, matrices, half_size)
        )
        half_size = half_size // 2
    skel_rows = skeleton.reshape(subtree, vec_count * rank)
    up = [(i, i + 1) for i in range(devices - 1)]
    down = [(j, i) for i, j in up]
    vecs = (lax.ppermute(vectors, AXES, up), vectors, lax.ppermute(vectors, AXES, down))
    xyz = (lax.ppermute(coords, AXES, up), coords, lax.ppermute(coords, AXES, down))
    skel_table = jnp.concatenate(
        [lax.ppermute(skel_rows, AXES, up), skel_rows, lax.ppermute(skel_rows, AXES, down)]
    )
    gathered = lax.all_gather(skel_rows[1:2], ("row", "col"), axis=0, tiled=True)
    top_mats = top_transfer.astype(jnp.float32).reshape(2 * devices, rank, rank)
    upper = jnp.zeros((2 * devices, vec_count, rank), jnp.float32)
    upper = upper.at[devices:].set(gathered.reshape(devices, vec_count, rank))
    half_size = devices // 2
    while half_size >= 2:
        upper = upper.at[half_size : 2 * half_size].set(upward_level(upper, top_mats, half_size))
        half_size = half_size // 2
    levels = devices.bit_length() - 1
    path_field = jnp.zeros((vec_count, rank), jnp.float32)
    for shift_bits in range(levels - 1, -1, -1):
        slot_now = devices + position >> shift_bits
        partners = upper[top_list[slot_now]]
        blocks = top_coupling[slot_now].astype(jnp.float32).reshape(top_count, rank, rank)
        own_part = jnp.einsum("kvr,krq->vq", partners, blocks, precision=HIGHEST_PREC)
        from_parent = jnp.einsum(
            "vq,rq->vr", path_field, top_mats[slot_now], precision=HIGHEST_PREC
        )
        path_field = own_part + from_parent
    local_ids = local_list - (position - 1) * subtree
    partners = skel_table[local_ids].reshape(subtree, far_count, vec_count, rank)
    blocks = coupling.astype(jnp.float32).reshape(subtree, far_count, rank, rank)
    field = jnp.einsum("skvr,skrq->svq", partners, blocks, precision=HIGHEST_PREC)
    field = field.at[0].set(0.0).at[1].set(path_field)
    half_size = 1
    while half_size < leaf_dev:
        field = downward_level(field, matrices, half_size)
        half_size = half_size * 2
    far_part = jnp.einsum("cvr,crl->vcl", field[leaf_dev:], basis, precision=HIGHEST_PREC)
    far = far_part.reshape(vec_count, leaf_dev * leaf_size)
    return near_call(near_list, near_count, vecs, xyz, far)


def solution(mesh):
    return jax.shard_map(
        per_device,
        mesh=mesh,
        in_specs=(
            P(None, ("row", "col")),
            P(None, ("row", "col")),
            P(("row", "col"), None, None),
            P(("row", "col"), None),
            P(("row", "col"), None, None),
            P(("row", "col"), None),
            P(("row", "col")),
            P(("row", "col"), None),
            P(),
            P(),
            P(),
        ),
        out_specs=P(None, ("row", "col")),
        check_vma=False,
    )
```

```python
import functools
import math

import jax
import jax.numpy as jnp
from jax import lax
from jax.experimental import pallas as pl
from jax.experimental.pallas import tpu as pltpu
from jax.sharding import PartitionSpec as P

ROOT_THREE = 1.7320508075688772
LENGTH_SCALE = 0.2
JITTER_SQ = 0.0001
LOG2E = 1.4426950408889634
MESH = pl.DeviceIdType.MESH
UNROLL = 4
F32 = jnp.float32
BF16 = jnp.bfloat16


def pieces(value, count):
    parts = []
    for _ in range(count):
        part = value.astype(BF16).astype(F32)
        parts.append(part)
        value = value - part
    return parts


def near_kernel(
    leaf_dev,
    ids_ref,
    count_ref,
    vec_refs,
    xyz_refs,
    far_ref,
    out_ref,
    own_feat,
    pair_feat,
    pair_vecs,
    pair_list,
):
    vec_count, width = out_ref.shape
    leaf = width // leaf_dev
    me = lax.axis_index("row") * lax.axis_size("col") + lax.axis_index("col")
    offset = (me - 1) * leaf_dev
    gain = ROOT_THREE / LENGTH_SCALE * LOG2E
    jitter = JITTER_SQ * gain * gain
    vec_gain = 1.0 / (LOG2E * math.sqrt(leaf))

    def list_leaf(c, total):
        def add(m, t):
            pair_list[0, t] = c
            pair_list[1, t] = ids_ref[c, m] - offset
            return t + 1

        return lax.fori_loop(0, count_ref[c], add, total)

    total = lax.fori_loop(0, leaf_dev, list_leaf, 0)
    for i in range(UNROLL):
        pair_list[0, total + i] = 0
        pair_list[1, total + i] = 3 * leaf_dev
    pair_vecs[3 * leaf_dev] = jnp.zeros((2 * vec_count, leaf), BF16)

    row_ids = lax.broadcasted_iota(jnp.int32, (8, leaf), 0)

    def build(part, c):
        cols = pl.ds(pl.multiple_of(c * leaf, leaf), leaf)
        xyz = (xyz_refs[part][:, cols] - 0.5) * gain
        norm = jnp.sum(xyz * xyz, axis=0, keepdims=True)
        wide = jnp.concatenate([xyz, jnp.zeros((5, leaf), F32)], axis=0)
        theirs = jnp.where(row_ids == 3, norm, jnp.where(row_ids == 4, 1.0, wide))
        b1, b2, b3 = pieces(theirs, 3)
        slot = part * leaf_dev + c
        pair_feat[slot] = jnp.concatenate([b1, b2, b1, b2, b3, b1], axis=0).astype(BF16)
        hi, lo = pieces(vec_refs[part][:, cols] * vec_gain, 2)
        pair_vecs[slot] = jnp.concatenate([hi, lo], axis=0).astype(BF16)
        if part == 1:
            mine = jnp.where(
                row_ids == 4, norm + jitter, jnp.where(row_ids == 3, 1.0, -2.0 * wide)
            )
            a1, a2, a3 = pieces(mine, 3)
            stacked = jnp.concatenate([a1, a1, a2, a2, a1, a3], axis=0)
            own_feat[c] = jnp.transpose(stacked).astype(BF16)

    for part in range(3):
        pl.loop(0, leaf_dev)(lambda c, part=part: build(part, c))
    pair_feat[3 * leaf_dev] = pair_feat[leaf_dev]

    out_ref[...] = far_ref[...]

    def pair(t):
        c, p = pair_list[0, t], pair_list[1, t]
        square = jnp.dot(own_feat[c], pair_feat[p], preferred_element_type=F32)
        dist = square * lax.rsqrt(square)
        matern = (LOG2E + dist) * jnp.exp2(-dist)
        high = matern.astype(BF16)
        low = (matern - high.astype(F32)).astype(BF16)
        vecs = pair_vecs[p]
        dims = (((1,), (1,)), ((), ()))
        first = lax.dot_general(vecs, high, dims, preferred_element_type=F32)
        second = lax.dot_general(vecs[:vec_count], low, dims, preferred_element_type=F32)
        return c, first[:vec_count] + first[vec_count:] + second

    @pl.loop(0, (total + UNROLL - 1) // UNROLL)
    def _(step):
        done = [pair(step * UNROLL + i) for i in range(UNROLL)]
        for c, added in done:
            cols = pl.ds(pl.multiple_of(c * leaf, leaf), leaf)
            out_ref[:, cols] += added


def near_call(near_list, near_count, vecs, xyz, far):
    leaf_dev, near = near_list.shape
    vec_count, width = far.shape
    leaf = width // leaf_dev

    def body(ids, count, v0, v1, v2, c0, c1, c2, far_ref, out_ref, *scratch):
        near_kernel(
            leaf_dev, ids, count, (v0, v1, v2), (c0, c1, c2), far_ref, out_ref, *scratch
        )

    vmem = pl.BlockSpec(memory_space=pltpu.VMEM)
    smem = pl.BlockSpec(memory_space=pltpu.SMEM)
    return pl.pallas_call(
        body,
        out_shape=jax.ShapeDtypeStruct((vec_count, width), F32),
        in_specs=[smem, smem] + [vmem] * 7,
        out_specs=vmem,
        scratch_shapes=[
            pltpu.VMEM((leaf_dev, leaf, 48), BF16),
            pltpu.VMEM((3 * leaf_dev + 1, 48, leaf), BF16),
            pltpu.VMEM((3 * leaf_dev + 1, 2 * vec_count, leaf), BF16),
            pltpu.SMEM((2, leaf_dev * near + UNROLL), jnp.int32),
        ],
        compiler_params=pltpu.CompilerParams(vmem_limit_bytes=48 * 1024 * 1024),
        cost_estimate=pl.CostEstimate(
            flops=2 * leaf_dev * near * leaf * leaf * 64,
            bytes_accessed=7 * 4 * vec_count * width,
            transcendentals=2 * leaf_dev * near * leaf * leaf,
        ),
        name="near_pairs",
    )(near_list, near_count, *vecs, *xyz, far)


def split_rows(value):
    return jnp.concatenate(pieces(value, 2), axis=0).astype(BF16)


def join_rows(value):
    half = value.shape[0] // 2
    return value[:half] + value[half:]


def dot_nn(left, right):
    return jnp.dot(left, right, preferred_element_type=F32)


def dot_nt(left, right):
    return lax.dot_general(left, right, (((1,), (1,)), ((), ())), preferred_element_type=F32)


def far_kernel(
    n_row,
    n_col,
    vec_ref,
    xyz_ref,
    basis_ref,
    transfer_ref,
    coupling_ref,
    list_ref,
    top_transfer_ref,
    top_coupling_ref,
    top_list_ref,
    far_ref,
    vec_prev,
    vec_next,
    xyz_prev,
    xyz_next,
    mats,
    couples,
    top_mats,
    top_couples,
    skel_own,
    skel_near,
    left_table,
    right_table,
    gathered,
    upper,
    field,
    near_send,
    near_recv,
    row_send,
    row_recv,
    col_send,
    col_recv,
):
    n = n_row * n_col
    row, col = lax.axis_index("row"), lax.axis_index("col")
    me = row * n_col + col
    leaf_dev, rank, leaf = basis_ref.shape
    vec_count = vec_ref.shape[0]
    subtree = 2 * leaf_dev
    far_count = coupling_ref.shape[1]
    top_count = top_coupling_ref.shape[1]
    lanes = 2 * rank
    chunks = transfer_ref.shape[1] // lanes
    has_prev, has_next = me > 0, me < n - 1
    prev_id = ((me + n - 1) % n // n_col, (me + n - 1) % n % n_col)
    next_id = ((me + 1) % n // n_col, (me + 1) % n % n_col)
    in_left = lax.broadcasted_iota(jnp.int32, (vec_count, lanes), 1) < rank

    def pick(even, odd):
        return jnp.where(in_left[: even.shape[0]], even, odd)

    barrier = pltpu.get_barrier_semaphore()
    for i in range(1, n_col):
        pl.semaphore_signal(
            barrier, inc=1, device_id=(row, (col + i) % n_col), device_id_type=MESH
        )
    for i in range(1, n_row):
        pl.semaphore_signal(
            barrier, inc=1, device_id=((row + i) % n_row, col), device_id_type=MESH
        )
    from_prev_row = jnp.logical_and(col == 0, has_prev)
    from_next_row = jnp.logical_and(col == n_col - 1, has_next)

    @pl.when(from_prev_row)
    def _():
        pl.semaphore_signal(barrier, inc=1, device_id=prev_id, device_id_type=MESH)

    @pl.when(from_next_row)
    def _():
        pl.semaphore_signal(barrier, inc=1, device_id=next_id, device_id_type=MESH)

    across = jnp.logical_or(from_prev_row, from_next_row)
    peers = n_col - 1 + n_row - 1

    @pl.when(across)
    def _():
        pl.semaphore_wait(barrier, peers + 1)

    @pl.when(jnp.logical_not(across))
    def _():
        pl.semaphore_wait(barrier, peers)

    def remote(src, dst, send, recv, target):
        return pltpu.make_async_remote_copy(
            src_ref=src,
            dst_ref=dst,
            send_sem=send,
            recv_sem=recv,
            device_id=target,
            device_id_type=MESH,
        )

    up = [
        remote(src, dst, near_send.at[i], near_recv.at[i], next_id)
        for i, (src, dst) in enumerate(
            [(vec_ref, vec_prev), (xyz_ref, xyz_prev), (skel_own, skel_near.at[0])]
        )
    ]
    down = [
        remote(src, dst, near_send.at[3 + i], near_recv.at[3 + i], prev_id)
        for i, (src, dst) in enumerate(
            [(vec_ref, vec_next), (xyz_ref, xyz_next), (skel_own, skel_near.at[1])]
        )
    ]

    def start_near(which):
        @pl.when(has_next)
        def _():
            for i in which:
                up[i].start()

        @pl.when(has_prev)
        def _():
            for i in which:
                down[i].start()

    def wait_near(which, sends):
        @pl.when(has_next)
        def _():
            for i in which:
                if sends:
                    up[i].wait_send()
                else:
                    down[i].wait_recv()

        @pl.when(has_prev)
        def _():
            for i in which:
                if sends:
                    down[i].wait_send()
                else:
                    up[i].wait_recv()

    start_near((0, 1))

    def unpack(chunk, dest, start, size):
        chunk = chunk.astype(F32)
        turned = pltpu.roll(chunk, rank, 1)
        low = lax.broadcasted_iota(jnp.int32, chunk.shape, 1) < rank
        dest[pl.ds(start, size, stride=rank), :] = jnp.where(low, chunk, turned)
        dest[pl.ds(start + 1, size, stride=rank), :] = jnp.where(low, turned, chunk)

    def unpack_slots(source, dest):
        slots = source.shape[0]

        @pl.loop(0, slots // 16)
        def _(block):
            rows = pl.ds(pl.multiple_of(block * 16, 16), 16)
            for k in range(chunks):
                chunk = source[rows, k * lanes : (k + 1) * lanes]
                unpack(chunk, dest, block * 16 * rank + 2 * k, 16)

    unpack_slots(transfer_ref, mats)

    def pair_mats(table, h):
        return table[pl.ds(pl.multiple_of(h * lanes, lanes), lanes), :].astype(BF16)

    def leaf_pair(h):
        return basis_ref[pl.ds(2 * h, 2)].reshape(lanes, leaf)

    @pl.loop(0, leaf_dev // 2, unroll=4)
    def _(i):
        cols = pl.ds(pl.multiple_of(2 * i * leaf, 2 * leaf), 2 * leaf)
        vecs = vec_ref[:, cols]
        parts = jnp.concatenate([split_rows(vecs[:, :leaf]), split_rows(vecs[:, leaf:])], axis=0)
        both = dot_nt(parts, leaf_pair(i))
        even, odd = both[: 2 * vec_count], both[2 * vec_count :]
        skel_own[leaf_dev // 2 + i] = pick(join_rows(even), join_rows(odd))

    def merged(pairs, table, h):
        return join_rows(dot_nn(split_rows(pairs[h]), pair_mats(table, h)))

    half = leaf_dev // 4
    while half >= 1:
        for h in range(half, 2 * half):
            skel_own[h] = pick(merged(skel_own, mats, 2 * h), merged(skel_own, mats, 2 * h + 1))
        half //= 2
    skel_own[0] = jnp.zeros((vec_count, lanes), F32)
    gathered[me] = merged(skel_own, mats, 1)

    start_near((2,))
    first = [
        remote(
            gathered.at[me], gathered.at[me], row_send.at[i], row_recv.at[i], (row, (col + i) % n_col)
        )
        for i in range(1, n_col)
    ]
    for copy in first:
        copy.start()

    unpack_slots(top_transfer_ref, top_mats)
    levels = n.bit_length() - 1
    for level in range(levels):
        slot = (n + me) // (1 << (levels - 1 - level))
        for k in range(chunks):
            chunk = top_coupling_ref[slot, :, k * lanes : (k + 1) * lanes]
            unpack(chunk, top_couples, level * top_count * rank + 2 * k, top_count)

    @pl.loop(2, subtree)
    def _(j):
        for k in range(chunks):
            chunk = coupling_ref[j, :, k * lanes : (k + 1) * lanes]
            unpack(chunk, couples, j * far_count * rank + 2 * k, far_count)

    def fill_tables(part, pairs):
        @pl.loop(1, leaf_dev, unroll=2)
        def _(h):
            pair = pairs[h]
            turned = pltpu.roll(pair, rank, 1)
            slot = part * subtree + 2 * h
            none = jnp.zeros_like(pair)
            left_table[slot] = split_rows(pick(pair, none))
            right_table[slot] = split_rows(pick(none, turned))
            left_table[slot + 1] = split_rows(pick(turned, none))
            right_table[slot + 1] = split_rows(pick(none, pair))

    fill_tables(1, skel_own)

    for i in range(1, n_col):
        source = (col + n_col - i) % n_col
        remote(
            gathered.at[me],
            gathered.at[row * n_col + source],
            row_send.at[i],
            row_recv.at[i],
            (row, source),
        ).wait_recv()
    own_row = gathered.at[pl.ds(row * n_col, n_col)]
    second = [
        remote(own_row, own_row, col_send.at[i], col_recv.at[i], ((row + i) % n_row, col))
        for i in range(1, n_row)
    ]
    for copy in second:
        copy.start()
    for i in range(1, n_row):
        source = (row + n_row - i) % n_row
        remote(
            own_row,
            gathered.at[pl.ds(source * n_col, n_col)],
            col_send.at[i],
            col_recv.at[i],
            (source, col),
        ).wait_recv()

    for d in range(n):
        upper[n + d] = gathered[d]
    half = n // 2
    while half >= 2:

        @pl.loop(half, 2 * half, unroll=2 if half == 2 else 4)
        def _(h):
            pair = split_rows(pick(upper[2 * h], upper[2 * h + 1]))
            upper[h] = join_rows(dot_nn(pair, pair_mats(top_mats, h)))

        half //= 2
    path = jnp.zeros((vec_count, lanes), F32)
    for level in range(levels):
        slot = (n + me) // (1 << (levels - 1 - level))
        partners = [upper[top_list_ref[slot, k]] for k in range(top_count)]
        own = jnp.zeros((vec_count, lanes), F32)
        for k in range(0, top_count, 2):
            block = top_couples[pl.ds((level * top_count + k) * rank, lanes), :].astype(BF16)
            own += join_rows(dot_nn(split_rows(pick(partners[k], partners[k + 1])), block))
        block = top_mats[pl.ds(pl.multiple_of(slot * rank, rank), rank), :].astype(BF16)
        block = jnp.concatenate([block, block], axis=0)
        parent = split_rows(pick(path, jnp.zeros_like(path)))
        path = own + join_rows(dot_nt(parent, block))

    wait_near((2,), False)

    @pl.when(has_prev)
    def _():
        fill_tables(0, skel_near.at[0])

    @pl.when(has_next)
    def _():
        fill_tables(2, skel_near.at[1])

    offset = (me - 1) * subtree

    def coupled(j):
        sides = []
        for k in range(0, far_count, 2):
            one, two = (jnp.clip(list_ref[j, i] - offset, 0, 3 * subtree - 1) for i in (k, k + 1))
            sides.append(left_table[one] + right_table[two])
        rows = pl.ds(pl.multiple_of(j * far_count * rank, lanes), far_count * rank)
        return join_rows(dot_nn(jnp.concatenate(sides, axis=1), couples[rows, :].astype(BF16)))

    @pl.loop(1, leaf_dev)
    def _(h):
        field[h] = pick(coupled(2 * h), coupled(2 * h + 1))

    none = jnp.zeros((vec_count, lanes), F32)

    def masked(j):
        pair = field[j // 2]
        return split_rows(pick(pair, none) if j % 2 == 0 else pick(none, pair))

    for h in range(1, leaf_dev):
        parent = split_rows(pick(path, none)) if h == 1 else masked(h)
        field[h] += join_rows(dot_nt(parent, pair_mats(mats, h)))

    @pl.loop(0, leaf_dev // 2, unroll=4)
    def _(i):
        pair = field[leaf_dev // 2 + i]
        sides = jnp.concatenate(
            [split_rows(pick(pair, none)), split_rows(pick(none, pair))], axis=0
        )
        both = dot_nn(sides, leaf_pair(i))
        even, odd = both[: 2 * vec_count], both[2 * vec_count :]
        cols = pl.ds(pl.multiple_of(2 * i * leaf, 2 * leaf), 2 * leaf)
        far_ref[:, cols] = jnp.concatenate([join_rows(even), join_rows(odd)], axis=1)

    for copy in first + second:
        copy.wait_send()
    wait_near((0, 1), False)
    wait_near((0, 1, 2), True)


def far_call(n_row, n_col, vectors, coords, basis, transfer, coupling, lists, tops):
    n = n_row * n_col
    leaf_dev, rank, _ = basis.shape
    vec_count, width = vectors.shape
    subtree, far_count, _ = coupling.shape
    top_count = tops[1].shape[1]
    lanes = 2 * rank
    levels = n.bit_length() - 1
    vmem = pl.BlockSpec(memory_space=pltpu.VMEM)
    smem = pl.BlockSpec(memory_space=pltpu.SMEM)
    hbm = pl.BlockSpec(memory_space=pl.ANY)
    shape = jax.ShapeDtypeStruct
    sems = pltpu.SemaphoreType.DMA

    def body(*refs):
        far_kernel(n_row, n_col, *refs)

    return pl.pallas_call(
        body,
        out_shape=[
            shape((vec_count, width), F32),
            shape((vec_count, width), F32),
            shape((vec_count, width), F32),
            shape(coords.shape, F32),
            shape(coords.shape, F32),
        ],
        in_specs=[vmem] * 5 + [smem] + [vmem] * 2 + [smem],
        out_specs=[vmem] + [hbm] * 4,
        scratch_shapes=[
            pltpu.VMEM((subtree * rank, lanes), F32),
            pltpu.VMEM((subtree * far_count * rank, lanes), F32),
            pltpu.VMEM((2 * n * rank, lanes), F32),
            pltpu.VMEM((levels * top_count * rank, lanes), F32),
            pltpu.VMEM((leaf_dev, vec_count, lanes), F32),
            pltpu.VMEM((2, leaf_dev, vec_count, lanes), F32),
            pltpu.VMEM((3 * subtree, 2 * vec_count, lanes), BF16),
            pltpu.VMEM((3 * subtree, 2 * vec_count, lanes), BF16),
            pltpu.VMEM((n, vec_count, lanes), F32),
            pltpu.VMEM((2 * n, vec_count, lanes), F32),
            pltpu.VMEM((leaf_dev, vec_count, lanes), F32),
            sems((6,)),
            sems((6,)),
            sems((n_col,)),
            sems((n_col,)),
            sems((n_row,)),
            sems((n_row,)),
        ],
        compiler_params=pltpu.CompilerParams(
            collective_id=0, has_side_effects=True, vmem_limit_bytes=56 * 1024 * 1024
        ),
        cost_estimate=pl.CostEstimate(
            flops=2 * 200 * 32 * lanes * lanes, bytes_accessed=10 * 1024 * 1024, transcendentals=0
        ),
        name="far_field",
    )(vectors, coords, basis, transfer, coupling, lists, *tops)


def per_device(
    n_row,
    n_col,
    vectors,
    coords,
    leaf_basis,
    transfer,
    coupling,
    near_list,
    near_count,
    local_list,
    top_transfer,
    top_coupling,
    top_list,
):
    far, vec_prev, vec_next, xyz_prev, xyz_next = far_call(
        n_row,
        n_col,
        vectors,
        coords,
        leaf_basis,
        transfer,
        coupling,
        local_list,
        (top_transfer, top_coupling, top_list),
    )
    vecs = (vec_prev, vectors, vec_next)
    xyz = (xyz_prev, coords, xyz_next)
    return near_call(near_list, near_count, vecs, xyz, far)


def solution(mesh):
    return jax.shard_map(
        functools.partial(per_device, mesh.shape["row"], mesh.shape["col"]),
        mesh=mesh,
        in_specs=(
            P(None, ("row", "col")),
            P(None, ("row", "col")),
            P(("row", "col"), None, None),
            P(("row", "col"), None),
            P(("row", "col"), None, None),
            P(("row", "col"), None),
            P(("row", "col")),
            P(("row", "col"), None),
            P(),
            P(),
            P(),
        ),
        out_specs=P(None, ("row", "col")),
        check_vma=False,
    )
```

```python
import functools
import math

import jax
import jax.numpy as jnp
from jax import lax
from jax.experimental import pallas as pl
from jax.experimental.pallas import tpu as pltpu
from jax.sharding import PartitionSpec as P

ROOT_THREE = 1.7320508075688772
LENGTH_SCALE = 0.2
JITTER_SQ = 0.0001
LOG2E = 1.4426950408889634
MESH = pl.DeviceIdType.MESH
UNROLL = 4
STRIP = 128
F32 = jnp.float32
BF16 = jnp.bfloat16


def pieces(value, count):
    parts = []
    for _ in range(count):
        part = value.astype(BF16).astype(F32)
        parts.append(part)
        value = value - part
    return parts


def near_kernel(
    leaf_dev,
    ids_ref,
    count_ref,
    vec_hbm,
    xyz_hbm,
    far_hbm,
    out_ref,
    own_feat,
    pair_feat,
    pair_vecs,
    pair_list,
    vec_refs,
    xyz_refs,
    load_sem,
):
    vec_count, width = out_ref.shape
    leaf = width // leaf_dev
    me = lax.axis_index("row") * lax.axis_size("col") + lax.axis_index("col")
    offset = (me - 1) * leaf_dev
    gain = ROOT_THREE / LENGTH_SCALE * LOG2E
    jitter = JITTER_SQ * gain * gain
    vec_gain = 1.0 / (LOG2E * math.sqrt(leaf))

    def load(src, dst, i):
        return pltpu.make_async_copy(src, dst, load_sem.at[i])

    loads = [load(vec_hbm[i], vec_refs.at[i], i) for i in range(3)]
    loads += [load(xyz_hbm[i], xyz_refs.at[i], 3 + i) for i in range(3)]
    loads += [load(far_hbm, out_ref, 6)]
    for i in (4, 1, 3, 0, 5, 2, 6):
        loads[i].start()

    def list_leaf(c, total):
        def add(m, t):
            pair_list[0, t] = c
            pair_list[1, t] = ids_ref[m, c] - offset
            return t + 1

        return lax.fori_loop(0, count_ref[c], add, total)

    total = lax.fori_loop(0, leaf_dev, list_leaf, 0)
    for i in range(UNROLL):
        pair_list[0, total + i] = 0
        pair_list[1, total + i] = 3 * leaf_dev
    pair_vecs[3 * leaf_dev] = jnp.zeros((2 * vec_count, leaf), BF16)

    row_ids = lax.broadcasted_iota(jnp.int32, (8, leaf), 0)

    def build(part, c):
        cols = pl.ds(pl.multiple_of(c * leaf, leaf), leaf)
        xyz = (xyz_refs[part, :, cols] - 0.5) * gain
        norm = jnp.sum(xyz * xyz, axis=0, keepdims=True)
        wide = jnp.concatenate([xyz, jnp.zeros((5, leaf), F32)], axis=0)
        theirs = jnp.where(row_ids == 3, norm, jnp.where(row_ids == 4, 1.0, wide))
        b1, b2, b3 = pieces(theirs, 3)
        slot = part * leaf_dev + c
        pair_feat[slot] = jnp.concatenate([b1, b2, b1, b2, b3, b1], axis=0).astype(BF16)
        hi, lo = pieces(vec_refs[part, :, cols] * vec_gain, 2)
        pair_vecs[slot] = jnp.concatenate([hi, lo], axis=0).astype(BF16)
        if part == 1:
            mine = jnp.where(
                row_ids == 4, norm + jitter, jnp.where(row_ids == 3, 1.0, -2.0 * wide)
            )
            a1, a2, a3 = pieces(mine, 3)
            stacked = jnp.concatenate([a1, a1, a2, a2, a1, a3], axis=0)
            own_feat[c] = jnp.transpose(stacked).astype(BF16)

    for part in (1, 0, 2):
        loads[3 + part].wait()
        loads[part].wait()
        pl.loop(0, leaf_dev, unroll=4)(lambda c, part=part: build(part, c))
    pair_feat[3 * leaf_dev] = pair_feat[leaf_dev]

    loads[6].wait()

    def pair(t):
        c, p = pair_list[0, t], pair_list[1, t]
        vecs = pair_vecs[p]
        dims = (((1,), (1,)), ((), ()))
        sums = []
        for start in range(0, leaf, STRIP):
            mine = own_feat[c, start : start + STRIP]
            square = jnp.dot(mine, pair_feat[p], preferred_element_type=F32)
            dist = square * lax.rsqrt(square)
            matern = (LOG2E + dist) * jnp.exp2(-dist)
            high = matern.astype(BF16)
            low = (matern - high.astype(F32)).astype(BF16)
            first = lax.dot_general(vecs, high, dims, preferred_element_type=F32)
            second = lax.dot_general(vecs[:vec_count], low, dims, preferred_element_type=F32)
            sums.append(first[:vec_count] + first[vec_count:] + second)
        return c, jnp.concatenate(sums, axis=1)

    @pl.loop(0, (total + UNROLL - 1) // UNROLL)
    def _(step):
        done = [pair(step * UNROLL + i) for i in range(UNROLL)]
        for c, added in done:
            cols = pl.ds(pl.multiple_of(c * leaf, leaf), leaf)
            out_ref[:, cols] += added


def near_call(near_list, near_count, vecs, xyz, far):
    near, leaf_dev = near_list.shape
    vec_count, width = far.shape
    leaf = width // leaf_dev

    def body(ids, count, v0, v1, v2, c0, c1, c2, far_ref, out_ref, *scratch):
        near_kernel(
            leaf_dev, ids, count, (v0, v1, v2), (c0, c1, c2), far_ref, out_ref, *scratch
        )

    vmem = pl.BlockSpec(memory_space=pltpu.VMEM)
    smem = pl.BlockSpec(memory_space=pltpu.SMEM)
    return pl.pallas_call(
        body,
        out_shape=jax.ShapeDtypeStruct((vec_count, width), F32),
        in_specs=[smem, smem] + [pl.BlockSpec(memory_space=pl.ANY)] * 7,
        out_specs=vmem,
        scratch_shapes=[
            pltpu.VMEM((leaf_dev, leaf, 48), BF16),
            pltpu.VMEM((3 * leaf_dev + 1, 48, leaf), BF16),
            pltpu.VMEM((3 * leaf_dev + 1, 2 * vec_count, leaf), BF16),
            pltpu.SMEM((2, leaf_dev * near + UNROLL), jnp.int32),
            pltpu.VMEM((3, vec_count, width), F32),
            pltpu.VMEM((3, 3, width), F32),
            pltpu.SemaphoreType.DMA((7,)),
        ],
        compiler_params=pltpu.CompilerParams(vmem_limit_bytes=48 * 1024 * 1024),
        cost_estimate=pl.CostEstimate(
            flops=2 * leaf_dev * near * leaf * leaf * 64,
            bytes_accessed=7 * 4 * vec_count * width,
            transcendentals=2 * leaf_dev * near * leaf * leaf,
        ),
        name="near_pairs",
    )(near_list, near_count, *vecs, *xyz, far)


def split_rows(value):
    return jnp.concatenate(pieces(value, 2), axis=0).astype(BF16)


def join_rows(value):
    half = value.shape[0] // 2
    return value[:half] + value[half:]


def dot_nn(left, right):
    return jnp.dot(left, right, preferred_element_type=F32)


def dot_nt(left, right):
    return lax.dot_general(left, right, (((1,), (1,)), ((), ())), preferred_element_type=F32)


def far_kernel(
    n_row,
    n_col,
    vec_ref,
    xyz_ref,
    basis_ref,
    transfer_hbm,
    coupling_hbm,
    list_ref,
    top_transfer_hbm,
    top_coupling_hbm,
    top_list_ref,
    far_ref,
    vec_prev,
    vec_next,
    xyz_prev,
    xyz_next,
    transfer_ref,
    coupling_ref,
    top_transfer_ref,
    top_coupling_ref,
    mats,
    couples,
    top_mats,
    top_couples,
    skel_own,
    skel_near,
    left_table,
    right_table,
    gathered,
    upper,
    field,
    near_send,
    near_recv,
    row_send,
    row_recv,
    col_send,
    col_recv,
    load_sem,
):
    n = n_row * n_col
    row, col = lax.axis_index("row"), lax.axis_index("col")
    me = row * n_col + col
    leaf_dev, rank, leaf = basis_ref.shape
    vec_count = vec_ref.shape[0]
    subtree = 2 * leaf_dev
    far_count = coupling_ref.shape[0]
    mat_rows, couple_rows = rank + 1, far_count * rank + 1
    top_count = top_coupling_ref.shape[1]
    lanes = 2 * rank
    chunks = transfer_ref.shape[1] // lanes
    has_prev, has_next = me > 0, me < n - 1
    prev_id = ((me + n - 1) % n // n_col, (me + n - 1) % n % n_col)
    next_id = ((me + 1) % n // n_col, (me + 1) % n % n_col)
    in_left = lax.broadcasted_iota(jnp.int32, (vec_count, lanes), 1) < rank

    def pick(even, odd):
        return jnp.where(in_left[: even.shape[0]], even, odd)

    loads = [
        pltpu.make_async_copy(src, dst, load_sem.at[i])
        for i, (src, dst) in enumerate(
            [
                (transfer_hbm, transfer_ref),
                (top_transfer_hbm, top_transfer_ref),
                (top_coupling_hbm, top_coupling_ref),
                (coupling_hbm, coupling_ref),
            ]
        )
    ]
    for load in loads:
        load.start()

    barrier = pltpu.get_barrier_semaphore()
    for i in range(1, n_col):
        pl.semaphore_signal(
            barrier, inc=1, device_id=(row, (col + i) % n_col), device_id_type=MESH
        )
    for i in range(1, n_row):
        pl.semaphore_signal(
            barrier, inc=1, device_id=((row + i) % n_row, col), device_id_type=MESH
        )
    from_prev_row = jnp.logical_and(col == 0, has_prev)
    from_next_row = jnp.logical_and(col == n_col - 1, has_next)

    @pl.when(from_prev_row)
    def _():
        pl.semaphore_signal(barrier, inc=1, device_id=prev_id, device_id_type=MESH)

    @pl.when(from_next_row)
    def _():
        pl.semaphore_signal(barrier, inc=1, device_id=next_id, device_id_type=MESH)

    across = jnp.logical_or(from_prev_row, from_next_row)
    peers = n_col - 1 + n_row - 1

    @pl.when(across)
    def _():
        pl.semaphore_wait(barrier, peers + 1)

    @pl.when(jnp.logical_not(across))
    def _():
        pl.semaphore_wait(barrier, peers)

    def remote(src, dst, send, recv, target):
        return pltpu.make_async_remote_copy(
            src_ref=src,
            dst_ref=dst,
            send_sem=send,
            recv_sem=recv,
            device_id=target,
            device_id_type=MESH,
        )

    up = [
        remote(src, dst, near_send.at[i], near_recv.at[i], next_id)
        for i, (src, dst) in enumerate(
            [(vec_ref, vec_prev), (xyz_ref, xyz_prev), (skel_own, skel_near.at[0])]
        )
    ]
    down = [
        remote(src, dst, near_send.at[3 + i], near_recv.at[3 + i], prev_id)
        for i, (src, dst) in enumerate(
            [(vec_ref, vec_next), (xyz_ref, xyz_next), (skel_own, skel_near.at[1])]
        )
    ]

    def start_near(which):
        @pl.when(has_next)
        def _():
            for i in which:
                up[i].start()

        @pl.when(has_prev)
        def _():
            for i in which:
                down[i].start()

    def wait_near(which, sends):
        @pl.when(has_next)
        def _():
            for i in which:
                if sends:
                    up[i].wait_send()
                else:
                    down[i].wait_recv()

        @pl.when(has_prev)
        def _():
            for i in which:
                if sends:
                    down[i].wait_send()
                else:
                    up[i].wait_recv()

    start_near((0, 1))

    def unpack(chunk, dest, start, size, stride):
        chunk = chunk.astype(F32)
        turned = pltpu.roll(chunk, rank, 1)
        low = lax.broadcasted_iota(jnp.int32, chunk.shape, 1) < rank
        dest[pl.ds(start, size, stride=stride), :] = jnp.where(low, chunk, turned)
        dest[pl.ds(start + 1, size, stride=stride), :] = jnp.where(low, turned, chunk)

    def unpack_slots(source, dest):
        slots = source.shape[0]

        @pl.loop(0, slots // 16)
        def _(block):
            rows = pl.ds(pl.multiple_of(block * 16, 16), 16)
            for k in range(chunks):
                chunk = source[rows, k * lanes : (k + 1) * lanes]
                unpack(chunk, dest, block * 16 * mat_rows + 2 * k, 16, mat_rows)

    loads[0].wait()
    unpack_slots(transfer_ref, mats)

    def pair_mats(table, h):
        even = table[pl.ds(2 * h * mat_rows, rank), :]
        odd = table[pl.ds((2 * h + 1) * mat_rows, rank), :]
        return jnp.concatenate([even, odd], axis=0).astype(BF16)

    def leaf_pair(h):
        return basis_ref[pl.ds(2 * h, 2)].reshape(lanes, leaf)

    @pl.loop(0, leaf_dev // 2, unroll=4)
    def _(i):
        cols = pl.ds(pl.multiple_of(2 * i * leaf, 2 * leaf), 2 * leaf)
        vecs = vec_ref[:, cols]
        parts = jnp.concatenate([split_rows(vecs[:, :leaf]), split_rows(vecs[:, leaf:])], axis=0)
        both = dot_nt(parts, leaf_pair(i))
        even, odd = both[: 2 * vec_count], both[2 * vec_count :]
        skel_own[leaf_dev // 2 + i] = pick(join_rows(even), join_rows(odd))

    def merged(pairs, table, h):
        return join_rows(dot_nn(split_rows(pairs[h]), pair_mats(table, h)))

    half = leaf_dev // 4
    while half >= 1:
        for h in range(half, 2 * half):
            skel_own[h] = pick(merged(skel_own, mats, 2 * h), merged(skel_own, mats, 2 * h + 1))
        half //= 2
    skel_own[0] = jnp.zeros((vec_count, lanes), F32)
    gathered[me] = merged(skel_own, mats, 1)

    start_near((2,))
    first = [
        remote(
            gathered.at[me], gathered.at[me], row_send.at[i], row_recv.at[i], (row, (col + i) % n_col)
        )
        for i in range(1, n_col)
    ]
    for copy in first:
        copy.start()

    for load in loads[1:]:
        load.wait()
    unpack_slots(top_transfer_ref, top_mats)
    levels = n.bit_length() - 1
    for level in range(levels):
        slot = (n + me) // (1 << (levels - 1 - level))
        for k in range(chunks):
            chunk = top_coupling_ref[slot, :, k * lanes : (k + 1) * lanes]
            unpack(chunk, top_couples, level * top_count * rank + 2 * k, top_count, rank)

    @pl.loop(0, subtree // 16 * far_count)
    def _(step):
        block, m = step // far_count, step % far_count
        rows = pl.ds(pl.multiple_of(block * 16, 16), 16)
        for k in range(chunks):
            chunk = coupling_ref[m, rows, k * lanes : (k + 1) * lanes]
            start = block * 16 * couple_rows + m * rank + 2 * k
            unpack(chunk, couples, start, 16, couple_rows)

    def fill_tables(part, pairs):
        @pl.loop(1, leaf_dev, unroll=2)
        def _(h):
            pair = pairs[h]
            turned = pltpu.roll(pair, rank, 1)
            slot = part * subtree + 2 * h
            none = jnp.zeros_like(pair)
            left_table[slot] = split_rows(pick(pair, none))
            right_table[slot] = split_rows(pick(none, turned))
            left_table[slot + 1] = split_rows(pick(turned, none))
            right_table[slot + 1] = split_rows(pick(none, pair))

    fill_tables(1, skel_own)

    for i in range(1, n_col):
        source = (col + n_col - i) % n_col
        remote(
            gathered.at[me],
            gathered.at[row * n_col + source],
            row_send.at[i],
            row_recv.at[i],
            (row, source),
        ).wait_recv()
    own_row = gathered.at[pl.ds(row * n_col, n_col)]
    second = [
        remote(own_row, own_row, col_send.at[i], col_recv.at[i], ((row + i) % n_row, col))
        for i in range(1, n_row)
    ]
    for copy in second:
        copy.start()
    for i in range(1, n_row):
        source = (row + n_row - i) % n_row
        remote(
            own_row,
            gathered.at[pl.ds(source * n_col, n_col)],
            col_send.at[i],
            col_recv.at[i],
            (source, col),
        ).wait_recv()

    for d in range(n):
        upper[n + d] = gathered[d]
    half = n // 2
    while half >= 2:

        @pl.loop(half, 2 * half, unroll=2 if half == 2 else 4)
        def _(h):
            pair = split_rows(pick(upper[2 * h], upper[2 * h + 1]))
            upper[h] = join_rows(dot_nn(pair, pair_mats(top_mats, h)))

        half //= 2
    path = jnp.zeros((vec_count, lanes), F32)
    for level in range(levels):
        slot = (n + me) // (1 << (levels - 1 - level))
        partners = [upper[top_list_ref[k, slot]] for k in range(top_count)]
        own = jnp.zeros((vec_count, lanes), F32)
        for k in range(0, top_count, 2):
            block = top_couples[pl.ds((level * top_count + k) * rank, lanes), :].astype(BF16)
            own += join_rows(dot_nn(split_rows(pick(partners[k], partners[k + 1])), block))
        block = top_mats[pl.ds(slot * mat_rows, rank), :].astype(BF16)
        block = jnp.concatenate([block, block], axis=0)
        parent = split_rows(pick(path, jnp.zeros_like(path)))
        path = own + join_rows(dot_nt(parent, block))

    wait_near((2,), False)

    @pl.when(has_prev)
    def _():
        fill_tables(0, skel_near.at[0])

    @pl.when(has_next)
    def _():
        fill_tables(2, skel_near.at[1])

    offset = (me - 1) * subtree

    def coupled(j):
        sides = []
        for k in range(0, far_count, 2):
            one, two = (jnp.clip(list_ref[i, j] - offset, 0, 3 * subtree - 1) for i in (k, k + 1))
            sides.append(left_table[one] + right_table[two])
        rows = pl.ds(j * couple_rows, far_count * rank)
        return join_rows(dot_nn(jnp.concatenate(sides, axis=1), couples[rows, :].astype(BF16)))

    @pl.loop(1, leaf_dev, unroll=2)
    def _(h):
        field[h] = pick(coupled(2 * h), coupled(2 * h + 1))

    none = jnp.zeros((vec_count, lanes), F32)

    def masked(j):
        pair = field[j // 2]
        return split_rows(pick(pair, none) if j % 2 == 0 else pick(none, pair))

    for h in range(1, leaf_dev):
        parent = split_rows(pick(path, none)) if h == 1 else masked(h)
        field[h] += join_rows(dot_nt(parent, pair_mats(mats, h)))

    @pl.loop(0, leaf_dev // 2, unroll=4)
    def _(i):
        pair = field[leaf_dev // 2 + i]
        sides = jnp.concatenate(
            [split_rows(pick(pair, none)), split_rows(pick(none, pair))], axis=0
        )
        both = dot_nn(sides, leaf_pair(i))
        even, odd = both[: 2 * vec_count], both[2 * vec_count :]
        cols = pl.ds(pl.multiple_of(2 * i * leaf, 2 * leaf), 2 * leaf)
        far_ref[:, cols] = jnp.concatenate([join_rows(even), join_rows(odd)], axis=1)

    for copy in first + second:
        copy.wait_send()
    wait_near((0, 1), False)
    wait_near((0, 1, 2), True)


def far_call(n_row, n_col, vectors, coords, basis, transfer, coupling, lists, tops):
    n = n_row * n_col
    leaf_dev, rank, _ = basis.shape
    vec_count, width = vectors.shape
    far_count, subtree, _ = coupling.shape
    top_count = tops[1].shape[1]
    lanes = 2 * rank
    levels = n.bit_length() - 1
    vmem = pl.BlockSpec(memory_space=pltpu.VMEM)
    smem = pl.BlockSpec(memory_space=pltpu.SMEM)
    hbm = pl.BlockSpec(memory_space=pl.ANY)
    shape = jax.ShapeDtypeStruct
    sems = pltpu.SemaphoreType.DMA

    def body(*refs):
        far_kernel(n_row, n_col, *refs)

    return pl.pallas_call(
        body,
        out_shape=[
            shape((vec_count, width), F32),
            shape((vec_count, width), F32),
            shape((vec_count, width), F32),
            shape(coords.shape, F32),
            shape(coords.shape, F32),
        ],
        in_specs=[vmem] * 3 + [hbm] * 2 + [smem] + [hbm] * 2 + [smem],
        out_specs=[vmem] + [hbm] * 4,
        scratch_shapes=[
            pltpu.VMEM(transfer.shape, BF16),
            pltpu.VMEM(coupling.shape, BF16),
            pltpu.VMEM(tops[0].shape, BF16),
            pltpu.VMEM(tops[1].shape, BF16),
            pltpu.VMEM((subtree * (rank + 1), lanes), F32),
            pltpu.VMEM((subtree * (far_count * rank + 1), lanes), F32),
            pltpu.VMEM((2 * n * (rank + 1), lanes), F32),
            pltpu.VMEM((levels * top_count * rank, lanes), F32),
            pltpu.VMEM((leaf_dev, vec_count, lanes), F32),
            pltpu.VMEM((2, leaf_dev, vec_count, lanes), F32),
            pltpu.VMEM((3 * subtree, 2 * vec_count, lanes), BF16),
            pltpu.VMEM((3 * subtree, 2 * vec_count, lanes), BF16),
            pltpu.VMEM((n, vec_count, lanes), F32),
            pltpu.VMEM((2 * n, vec_count, lanes), F32),
            pltpu.VMEM((leaf_dev, vec_count, lanes), F32),
            sems((6,)),
            sems((6,)),
            sems((n_col,)),
            sems((n_col,)),
            sems((n_row,)),
            sems((n_row,)),
            sems((4,)),
        ],
        compiler_params=pltpu.CompilerParams(
            collective_id=0, has_side_effects=True, vmem_limit_bytes=56 * 1024 * 1024
        ),
        cost_estimate=pl.CostEstimate(
            flops=2 * 200 * 32 * lanes * lanes, bytes_accessed=10 * 1024 * 1024, transcendentals=0
        ),
        name="far_field",
    )(vectors, coords, basis, transfer, coupling, lists, *tops)


def per_device(
    n_row,
    n_col,
    vectors,
    coords,
    leaf_basis,
    transfer,
    coupling,
    near_list,
    near_count,
    local_list,
    top_transfer,
    top_coupling,
    top_list,
):
    far, vec_prev, vec_next, xyz_prev, xyz_next = far_call(
        n_row,
        n_col,
        vectors,
        coords,
        leaf_basis,
        transfer,
        jnp.transpose(coupling, (1, 0, 2)),
        jnp.transpose(local_list),
        (top_transfer, top_coupling, jnp.transpose(top_list)),
    )
    vecs = (vec_prev, vectors, vec_next)
    xyz = (xyz_prev, coords, xyz_next)
    return near_call(jnp.transpose(near_list), near_count, vecs, xyz, far)


def solution(mesh):
    return jax.shard_map(
        functools.partial(per_device, mesh.shape["row"], mesh.shape["col"]),
        mesh=mesh,
        in_specs=(
            P(None, ("row", "col")),
            P(None, ("row", "col")),
            P(("row", "col"), None, None),
            P(("row", "col"), None),
            P(("row", "col"), None, None),
            P(("row", "col"), None),
            P(("row", "col")),
            P(("row", "col"), None),
            P(),
            P(),
            P(),
        ),
        out_specs=P(None, ("row", "col")),
        check_vma=False,
    )
```

```python
import functools
import math

import jax
import jax.numpy as jnp
from jax import lax
from jax.experimental import pallas as pl
from jax.experimental.pallas import tpu as pltpu
from jax.sharding import PartitionSpec as P

ROOT_THREE = 1.7320508075688772
LENGTH_SCALE = 0.2
JITTER_SQ = 0.0001
LOG2E = 1.4426950408889634
MESH = pl.DeviceIdType.MESH
UNROLL = 4
F32 = jnp.float32
BF16 = jnp.bfloat16


def pieces(value, count):
    parts = []
    for _ in range(count):
        part = value.astype(BF16).astype(F32)
        parts.append(part)
        value = value - part
    return parts


def near_kernel(
    leaf_dev,
    ids_ref,
    count_ref,
    vec_hbm,
    xyz_hbm,
    far_hbm,
    out_ref,
    own_feat,
    pair_feat,
    pair_vecs,
    pair_list,
    vec_refs,
    xyz_refs,
    load_sem,
    ahead,
):
    vec_count, width = out_ref.shape
    leaf = width // leaf_dev
    me = lax.axis_index("row") * lax.axis_size("col") + lax.axis_index("col")
    offset = (me - 1) * leaf_dev
    gain = ROOT_THREE / LENGTH_SCALE * LOG2E
    jitter = JITTER_SQ * gain * gain
    vec_gain = 1.0 / (LOG2E * math.sqrt(leaf))

    def load(src, dst, i):
        return pltpu.make_async_copy(src, dst, load_sem.at[i])

    loads = [load(vec_hbm[i], vec_refs.at[i], i) for i in range(3)]
    loads += [load(xyz_hbm[i], xyz_refs.at[i], 3 + i) for i in range(3)]
    loads += [load(far_hbm, out_ref, 6)]
    for i in (4, 1, 3, 0, 5, 2, 6):
        loads[i].start()

    def list_leaf(c, total):
        def add(m, t):
            pair_list[0, t] = c
            pair_list[1, t] = ids_ref[m, c] - offset
            return t + 1

        return lax.fori_loop(0, count_ref[c], add, total)

    total = lax.fori_loop(0, leaf_dev, list_leaf, 0)
    for i in range(UNROLL + 1):
        pair_list[0, total + i] = 0
        pair_list[1, total + i] = 3 * leaf_dev
    pair_vecs[3 * leaf_dev] = jnp.zeros((2 * vec_count, leaf), BF16)

    row_ids = lax.broadcasted_iota(jnp.int32, (8, leaf), 0)

    def build(part, c):
        cols = pl.ds(pl.multiple_of(c * leaf, leaf), leaf)
        xyz = (xyz_refs[part, :, cols] - 0.5) * gain
        norm = jnp.sum(xyz * xyz, axis=0, keepdims=True)
        wide = jnp.concatenate([xyz, jnp.zeros((5, leaf), F32)], axis=0)
        theirs = jnp.where(row_ids == 3, norm, jnp.where(row_ids == 4, 1.0, wide))
        b1, b2, b3 = pieces(theirs, 3)
        slot = part * leaf_dev + c
        pair_feat[slot] = jnp.concatenate([b1, b2, b1, b2, b3, b1], axis=0).astype(BF16)
        hi, lo = pieces(vec_refs[part, :, cols] * vec_gain, 2)
        pair_vecs[slot] = jnp.concatenate([hi, lo], axis=0).astype(BF16)
        if part == 1:
            mine = jnp.where(
                row_ids == 4, norm + jitter, jnp.where(row_ids == 3, 1.0, -2.0 * wide)
            )
            a1, a2, a3 = pieces(mine, 3)
            stacked = jnp.concatenate([a1, a1, a2, a2, a1, a3], axis=0)
            own_feat[c] = jnp.transpose(stacked).astype(BF16)

    for part in (1, 0, 2):
        loads[3 + part].wait()
        loads[part].wait()
        pl.loop(0, leaf_dev, unroll=4)(lambda c, part=part: build(part, c))
    pair_feat[3 * leaf_dev] = pair_feat[leaf_dev]

    loads[6].wait()

    def squares(t):
        mine, theirs = own_feat[pair_list[0, t]], pair_feat[pair_list[1, t]]
        return jnp.dot(mine, theirs, preferred_element_type=F32)

    def summed(t, square):
        dist = square * lax.rsqrt(square)
        matern = (LOG2E + dist) * jnp.exp2(-dist)
        high = matern.astype(BF16)
        low = (matern - high.astype(F32)).astype(BF16)
        vecs = pair_vecs[pair_list[1, t]]
        both = lax.dot_general(
            jnp.concatenate([vecs, vecs], axis=1),
            jnp.concatenate([high, low], axis=1),
            (((1,), (1,)), ((), ())),
            preferred_element_type=F32,
        )
        return both[:vec_count] + both[vec_count:]

    ahead[...] = squares(0)

    @pl.loop(0, (total + UNROLL - 1) // UNROLL)
    def _(step):
        square = ahead[...]
        done = []
        for i in range(UNROLL):
            t = step * UNROLL + i
            following = squares(t + 1)
            done.append(summed(t, square))
            square = following
        ahead[...] = square
        for i, added in enumerate(done):
            c = pair_list[0, step * UNROLL + i]
            cols = pl.ds(pl.multiple_of(c * leaf, leaf), leaf)
            out_ref[:, cols] += added


def near_call(near_list, near_count, vecs, xyz, far):
    near, leaf_dev = near_list.shape
    vec_count, width = far.shape
    leaf = width // leaf_dev

    def body(ids, count, v0, v1, v2, c0, c1, c2, far_ref, out_ref, *scratch):
        near_kernel(
            leaf_dev, ids, count, (v0, v1, v2), (c0, c1, c2), far_ref, out_ref, *scratch
        )

    vmem = pl.BlockSpec(memory_space=pltpu.VMEM)
    smem = pl.BlockSpec(memory_space=pltpu.SMEM)
    return pl.pallas_call(
        body,
        out_shape=jax.ShapeDtypeStruct((vec_count, width), F32),
        in_specs=[smem, smem] + [pl.BlockSpec(memory_space=pl.ANY)] * 7,
        out_specs=vmem,
        scratch_shapes=[
            pltpu.VMEM((leaf_dev, leaf, 48), BF16),
            pltpu.VMEM((3 * leaf_dev + 1, 48, leaf), BF16),
            pltpu.VMEM((3 * leaf_dev + 1, 2 * vec_count, leaf), BF16),
            pltpu.SMEM((2, leaf_dev * near + UNROLL + 1), jnp.int32),
            pltpu.VMEM((3, vec_count, width), F32),
            pltpu.VMEM((3, 3, width), F32),
            pltpu.SemaphoreType.DMA((7,)),
            pltpu.VMEM((leaf, leaf), F32),
        ],
        compiler_params=pltpu.CompilerParams(vmem_limit_bytes=60 * 1024 * 1024),
        cost_estimate=pl.CostEstimate(
            flops=2 * leaf_dev * near * leaf * leaf * 64,
            bytes_accessed=7 * 4 * vec_count * width,
            transcendentals=2 * leaf_dev * near * leaf * leaf,
        ),
        name="near_pairs",
    )(near_list, near_count, *vecs, *xyz, far)


def split_rows(value):
    return jnp.concatenate(pieces(value, 2), axis=0).astype(BF16)


def join_rows(value):
    half = value.shape[0] // 2
    return value[:half] + value[half:]


def dot_nn(left, right):
    return jnp.dot(left, right, preferred_element_type=F32)


def dot_nt(left, right):
    return lax.dot_general(left, right, (((1,), (1,)), ((), ())), preferred_element_type=F32)


def far_kernel(
    n_row,
    n_col,
    vec_ref,
    xyz_ref,
    basis_ref,
    transfer_hbm,
    coupling_hbm,
    list_ref,
    top_transfer_hbm,
    top_coupling_hbm,
    top_list_ref,
    far_ref,
    vec_prev,
    vec_next,
    xyz_prev,
    xyz_next,
    transfer_ref,
    coupling_ref,
    top_transfer_ref,
    top_coupling_ref,
    mats,
    couples,
    top_mats,
    top_couples,
    skel_own,
    skel_near,
    left_table,
    right_table,
    gathered,
    upper,
    field,
    near_send,
    near_recv,
    row_send,
    row_recv,
    col_send,
    col_recv,
    load_sem,
):
    n = n_row * n_col
    row, col = lax.axis_index("row"), lax.axis_index("col")
    me = row * n_col + col
    leaf_dev, rank, leaf = basis_ref.shape
    vec_count = vec_ref.shape[0]
    subtree = 2 * leaf_dev
    far_count = coupling_ref.shape[0]
    mat_rows, couple_rows = rank + 1, far_count * rank + 1
    top_count = top_coupling_ref.shape[1]
    lanes = 2 * rank
    chunks = transfer_ref.shape[1] // lanes
    has_prev, has_next = me > 0, me < n - 1
    prev_id = ((me + n - 1) % n // n_col, (me + n - 1) % n % n_col)
    next_id = ((me + 1) % n // n_col, (me + 1) % n % n_col)
    in_left = lax.broadcasted_iota(jnp.int32, (vec_count, lanes), 1) < rank

    def pick(even, odd):
        return jnp.where(in_left[: even.shape[0]], even, odd)

    loads = [
        pltpu.make_async_copy(src, dst, load_sem.at[i])
        for i, (src, dst) in enumerate(
            [
                (transfer_hbm, transfer_ref),
                (top_transfer_hbm, top_transfer_ref),
                (top_coupling_hbm, top_coupling_ref),
                (coupling_hbm, coupling_ref),
            ]
        )
    ]
    for load in loads:
        load.start()

    barrier = pltpu.get_barrier_semaphore()
    for i in range(1, n_col):
        pl.semaphore_signal(
            barrier, inc=1, device_id=(row, (col + i) % n_col), device_id_type=MESH
        )
    for i in range(1, n_row):
        pl.semaphore_signal(
            barrier, inc=1, device_id=((row + i) % n_row, col), device_id_type=MESH
        )
    from_prev_row = jnp.logical_and(col == 0, has_prev)
    from_next_row = jnp.logical_and(col == n_col - 1, has_next)

    @pl.when(from_prev_row)
    def _():
        pl.semaphore_signal(barrier, inc=1, device_id=prev_id, device_id_type=MESH)

    @pl.when(from_next_row)
    def _():
        pl.semaphore_signal(barrier, inc=1, device_id=next_id, device_id_type=MESH)

    across = jnp.logical_or(from_prev_row, from_next_row)
    peers = n_col - 1 + n_row - 1

    @pl.when(across)
    def _():
        pl.semaphore_wait(barrier, peers + 1)

    @pl.when(jnp.logical_not(across))
    def _():
        pl.semaphore_wait(barrier, peers)

    def remote(src, dst, send, recv, target):
        return pltpu.make_async_remote_copy(
            src_ref=src,
            dst_ref=dst,
            send_sem=send,
            recv_sem=recv,
            device_id=target,
            device_id_type=MESH,
        )

    up = [
        remote(src, dst, near_send.at[i], near_recv.at[i], next_id)
        for i, (src, dst) in enumerate(
            [(vec_ref, vec_prev), (xyz_ref, xyz_prev), (skel_own, skel_near.at[0])]
        )
    ]
    down = [
        remote(src, dst, near_send.at[3 + i], near_recv.at[3 + i], prev_id)
        for i, (src, dst) in enumerate(
            [(vec_ref, vec_next), (xyz_ref, xyz_next), (skel_own, skel_near.at[1])]
        )
    ]

    def start_near(which):
        @pl.when(has_next)
        def _():
            for i in which:
                up[i].start()

        @pl.when(has_prev)
        def _():
            for i in which:
                down[i].start()

    def wait_near(which, sends):
        @pl.when(has_next)
        def _():
            for i in which:
                if sends:
                    up[i].wait_send()
                else:
                    down[i].wait_recv()

        @pl.when(has_prev)
        def _():
            for i in which:
                if sends:
                    down[i].wait_send()
                else:
                    up[i].wait_recv()

    start_near((0, 1))

    def unpack(chunk, dest, start, size, stride):
        chunk = chunk.astype(F32)
        turned = pltpu.roll(chunk, rank, 1)
        low = lax.broadcasted_iota(jnp.int32, chunk.shape, 1) < rank
        dest[pl.ds(start, size, stride=stride), :] = jnp.where(low, chunk, turned)
        dest[pl.ds(start + 1, size, stride=stride), :] = jnp.where(low, turned, chunk)

    def unpack_slots(source, dest):
        slots = source.shape[0]

        @pl.loop(0, slots // 16)
        def _(block):
            rows = pl.ds(pl.multiple_of(block * 16, 16), 16)
            for k in range(chunks):
                chunk = source[rows, k * lanes : (k + 1) * lanes]
                unpack(chunk, dest, block * 16 * mat_rows + 2 * k, 16, mat_rows)

    loads[0].wait()
    unpack_slots(transfer_ref, mats)

    def pair_mats(table, h):
        even = table[pl.ds(2 * h * mat_rows, rank), :]
        odd = table[pl.ds((2 * h + 1) * mat_rows, rank), :]
        return jnp.concatenate([even, odd], axis=0).astype(BF16)

    def leaf_pair(h):
        return basis_ref[pl.ds(2 * h, 2)].reshape(lanes, leaf)

    @pl.loop(0, leaf_dev // 2, unroll=4)
    def _(i):
        cols = pl.ds(pl.multiple_of(2 * i * leaf, 2 * leaf), 2 * leaf)
        vecs = vec_ref[:, cols]
        parts = jnp.concatenate([split_rows(vecs[:, :leaf]), split_rows(vecs[:, leaf:])], axis=0)
        both = dot_nt(parts, leaf_pair(i))
        even, odd = both[: 2 * vec_count], both[2 * vec_count :]
        skel_own[leaf_dev // 2 + i] = pick(join_rows(even), join_rows(odd))

    def two_products(one, two, left, right):
        both = dot_nn(jnp.concatenate([one, two], axis=0), jnp.concatenate([left, right], axis=1))
        rows = one.shape[0]
        return join_rows(both[:rows, :lanes]), join_rows(both[rows:, lanes:])

    half = leaf_dev // 4
    while half >= 1:
        for h in range(half, 2 * half):
            skel_own[h] = pick(
                *two_products(
                    split_rows(skel_own[2 * h]),
                    split_rows(skel_own[2 * h + 1]),
                    pair_mats(mats, 2 * h),
                    pair_mats(mats, 2 * h + 1),
                )
            )
        half //= 2
    skel_own[0] = jnp.zeros((vec_count, lanes), F32)
    gathered[me] = join_rows(dot_nn(split_rows(skel_own[1]), pair_mats(mats, 1)))

    start_near((2,))
    first = [
        remote(
            gathered.at[me], gathered.at[me], row_send.at[i], row_recv.at[i], (row, (col + i) % n_col)
        )
        for i in range(1, n_col)
    ]
    for copy in first:
        copy.start()

    for load in loads[1:]:
        load.wait()
    unpack_slots(top_transfer_ref, top_mats)
    levels = n.bit_length() - 1
    for level in range(levels):
        slot = (n + me) // (1 << (levels - 1 - level))
        for k in range(chunks):
            chunk = top_coupling_ref[slot, :, k * lanes : (k + 1) * lanes]
            unpack(chunk, top_couples, level * top_count * rank + 2 * k, top_count, rank)

    @pl.loop(0, subtree // 16 * far_count)
    def _(step):
        block, m = step // far_count, step % far_count
        rows = pl.ds(pl.multiple_of(block * 16, 16), 16)
        for k in range(chunks):
            chunk = coupling_ref[m, rows, k * lanes : (k + 1) * lanes]
            start = block * 16 * couple_rows + m * rank + 2 * k
            unpack(chunk, couples, start, 16, couple_rows)

    def fill_tables(part, pairs):
        @pl.loop(1, leaf_dev, unroll=2)
        def _(h):
            pair = pairs[h]
            turned = pltpu.roll(pair, rank, 1)
            slot = part * subtree + 2 * h
            none = jnp.zeros_like(pair)
            left_table[slot] = split_rows(pick(pair, none))
            right_table[slot] = split_rows(pick(none, turned))
            left_table[slot + 1] = split_rows(pick(turned, none))
            right_table[slot + 1] = split_rows(pick(none, pair))

    fill_tables(1, skel_own)

    for i in range(1, n_col):
        source = (col + n_col - i) % n_col
        remote(
            gathered.at[me],
            gathered.at[row * n_col + source],
            row_send.at[i],
            row_recv.at[i],
            (row, source),
        ).wait_recv()
    own_row = gathered.at[pl.ds(row * n_col, n_col)]
    second = [
        remote(own_row, own_row, col_send.at[i], col_recv.at[i], ((row + i) % n_row, col))
        for i in range(1, n_row)
    ]
    for copy in second:
        copy.start()
    for i in range(1, n_row):
        source = (row + n_row - i) % n_row
        remote(
            own_row,
            gathered.at[pl.ds(source * n_col, n_col)],
            col_send.at[i],
            col_recv.at[i],
            (source, col),
        ).wait_recv()

    for d in range(n):
        upper[n + d] = gathered[d]
    half = n // 2
    while half >= 2:

        @pl.loop(half // 2, half, unroll=1 if half == 2 else 2)
        def _(g):
            h = 2 * g
            one = split_rows(pick(upper[2 * h], upper[2 * h + 1]))
            two = split_rows(pick(upper[2 * h + 2], upper[2 * h + 3]))
            upper[h], upper[h + 1] = two_products(
                one, two, pair_mats(top_mats, h), pair_mats(top_mats, h + 1)
            )

        half //= 2
    path = jnp.zeros((vec_count, lanes), F32)
    for level in range(levels):
        slot = (n + me) // (1 << (levels - 1 - level))
        partners = [upper[top_list_ref[k, slot]] for k in range(top_count)]
        own = jnp.zeros((vec_count, lanes), F32)
        for k in range(0, top_count, 2):
            block = top_couples[pl.ds((level * top_count + k) * rank, lanes), :].astype(BF16)
            own += join_rows(dot_nn(split_rows(pick(partners[k], partners[k + 1])), block))
        block = top_mats[pl.ds(slot * mat_rows, rank), :].astype(BF16)
        block = jnp.concatenate([block, block], axis=0)
        parent = split_rows(pick(path, jnp.zeros_like(path)))
        path = own + join_rows(dot_nt(parent, block))

    wait_near((2,), False)

    @pl.when(has_prev)
    def _():
        fill_tables(0, skel_near.at[0])

    @pl.when(has_next)
    def _():
        fill_tables(2, skel_near.at[1])

    offset = (me - 1) * subtree

    def coupled(j):
        sides = []
        for k in range(0, far_count, 2):
            one, two = (jnp.clip(list_ref[i, j] - offset, 0, 3 * subtree - 1) for i in (k, k + 1))
            sides.append(left_table[one] + right_table[two])
        rows = pl.ds(j * couple_rows, far_count * rank)
        return jnp.concatenate(sides, axis=1), couples[rows, :].astype(BF16)

    @pl.loop(1, leaf_dev, unroll=2)
    def _(h):
        (one, left), (two, right) = coupled(2 * h), coupled(2 * h + 1)
        field[h] = pick(*two_products(one, two, left, right))

    none = jnp.zeros((vec_count, lanes), F32)

    def masked(j):
        pair = field[j // 2]
        return split_rows(pick(pair, none) if j % 2 == 0 else pick(none, pair))

    field[1] += join_rows(dot_nt(split_rows(pick(path, none)), pair_mats(mats, 1)))
    for h in range(2, leaf_dev, 2):
        parents = jnp.concatenate([masked(h), masked(h + 1)], axis=0)
        blocks = jnp.concatenate([pair_mats(mats, h), pair_mats(mats, h + 1)], axis=0)
        both = dot_nt(parents, blocks)
        field[h] += join_rows(both[: 2 * vec_count, :lanes])
        field[h + 1] += join_rows(both[2 * vec_count :, lanes:])

    @pl.loop(0, leaf_dev // 2, unroll=4)
    def _(i):
        pair = field[leaf_dev // 2 + i]
        sides = jnp.concatenate(
            [split_rows(pick(pair, none)), split_rows(pick(none, pair))], axis=0
        )
        both = dot_nn(sides, leaf_pair(i))
        even, odd = both[: 2 * vec_count], both[2 * vec_count :]
        cols = pl.ds(pl.multiple_of(2 * i * leaf, 2 * leaf), 2 * leaf)
        far_ref[:, cols] = jnp.concatenate([join_rows(even), join_rows(odd)], axis=1)

    for copy in first + second:
        copy.wait_send()
    wait_near((0, 1), False)
    wait_near((0, 1, 2), True)


def far_call(n_row, n_col, vectors, coords, basis, transfer, coupling, lists, tops):
    n = n_row * n_col
    leaf_dev, rank, _ = basis.shape
    vec_count, width = vectors.shape
    far_count, subtree, _ = coupling.shape
    top_count = tops[1].shape[1]
    lanes = 2 * rank
    levels = n.bit_length() - 1
    vmem = pl.BlockSpec(memory_space=pltpu.VMEM)
    smem = pl.BlockSpec(memory_space=pltpu.SMEM)
    hbm = pl.BlockSpec(memory_space=pl.ANY)
    shape = jax.ShapeDtypeStruct
    sems = pltpu.SemaphoreType.DMA

    def body(*refs):
        far_kernel(n_row, n_col, *refs)

    return pl.pallas_call(
        body,
        out_shape=[
            shape((vec_count, width), F32),
            shape((vec_count, width), F32),
            shape((vec_count, width), F32),
            shape(coords.shape, F32),
            shape(coords.shape, F32),
        ],
        in_specs=[vmem] * 3 + [hbm] * 2 + [smem] + [hbm] * 2 + [smem],
        out_specs=[vmem] + [hbm] * 4,
        scratch_shapes=[
            pltpu.VMEM(transfer.shape, BF16),
            pltpu.VMEM(coupling.shape, BF16),
            pltpu.VMEM(tops[0].shape, BF16),
            pltpu.VMEM(tops[1].shape, BF16),
            pltpu.VMEM((subtree * (rank + 1), lanes), F32),
            pltpu.VMEM((subtree * (far_count * rank + 1), lanes), F32),
            pltpu.VMEM((2 * n * (rank + 1), lanes), F32),
            pltpu.VMEM((levels * top_count * rank, lanes), F32),
            pltpu.VMEM((leaf_dev, vec_count, lanes), F32),
            pltpu.VMEM((2, leaf_dev, vec_count, lanes), F32),
            pltpu.VMEM((3 * subtree, 2 * vec_count, lanes), BF16),
            pltpu.VMEM((3 * subtree, 2 * vec_count, lanes), BF16),
            pltpu.VMEM((n, vec_count, lanes), F32),
            pltpu.VMEM((2 * n, vec_count, lanes), F32),
            pltpu.VMEM((leaf_dev, vec_count, lanes), F32),
            sems((6,)),
            sems((6,)),
            sems((n_col,)),
            sems((n_col,)),
            sems((n_row,)),
            sems((n_row,)),
            sems((4,)),
        ],
        compiler_params=pltpu.CompilerParams(
            collective_id=0, has_side_effects=True, vmem_limit_bytes=60 * 1024 * 1024
        ),
        cost_estimate=pl.CostEstimate(
            flops=2 * 200 * 32 * lanes * lanes, bytes_accessed=10 * 1024 * 1024, transcendentals=0
        ),
        name="far_field",
    )(vectors, coords, basis, transfer, coupling, lists, *tops)


def per_device(
    n_row,
    n_col,
    vectors,
    coords,
    leaf_basis,
    transfer,
    coupling,
    near_list,
    near_count,
    local_list,
    top_transfer,
    top_coupling,
    top_list,
):
    far, vec_prev, vec_next, xyz_prev, xyz_next = far_call(
        n_row,
        n_col,
        vectors,
        coords,
        leaf_basis,
        transfer,
        jnp.transpose(coupling, (1, 0, 2)),
        jnp.transpose(local_list),
        (top_transfer, top_coupling, jnp.transpose(top_list)),
    )
    vecs = (vec_prev, vectors, vec_next)
    xyz = (xyz_prev, coords, xyz_next)
    return near_call(jnp.transpose(near_list), near_count, vecs, xyz, far)


def solution(mesh):
    return jax.shard_map(
        functools.partial(per_device, mesh.shape["row"], mesh.shape["col"]),
        mesh=mesh,
        in_specs=(
            P(None, ("row", "col")),
            P(None, ("row", "col")),
            P(("row", "col"), None, None),
            P(("row", "col"), None),
            P(("row", "col"), None, None),
            P(("row", "col"), None),
            P(("row", "col")),
            P(("row", "col"), None),
            P(),
            P(),
            P(),
        ),
        out_specs=P(None, ("row", "col")),
        check_vma=False,
    )
```

```python
import functools
import math

import jax
import jax.numpy as jnp
from jax import lax
from jax.experimental import pallas as pl
from jax.experimental.pallas import tpu as pltpu
from jax.sharding import PartitionSpec as P

ROOT_THREE = 1.7320508075688772
LENGTH_SCALE = 0.2
JITTER_SQ = 0.0001
LOG2E = 1.4426950408889634
MESH = pl.DeviceIdType.MESH
UNROLL = 4
F32 = jnp.float32
BF16 = jnp.bfloat16


def pieces(value, count):
    parts = []
    for _ in range(count):
        part = value.astype(BF16).astype(F32)
        parts.append(part)
        value = value - part
    return parts


def near_kernel(
    leaf_dev,
    ids_ref,
    count_ref,
    vec_hbm,
    xyz_hbm,
    far_hbm,
    out_ref,
    own_feat,
    pair_feat,
    pair_vecs,
    pair_list,
    vec_refs,
    xyz_refs,
    load_sem,
    ahead,
):
    vec_count, width = out_ref.shape
    leaf = width // leaf_dev
    me = lax.axis_index("row") * lax.axis_size("col") + lax.axis_index("col")
    offset = (me - 1) * leaf_dev
    gain = ROOT_THREE / LENGTH_SCALE * LOG2E
    jitter = JITTER_SQ * gain * gain
    vec_gain = 1.0 / (LOG2E * math.sqrt(leaf))

    def load(src, dst, i):
        return pltpu.make_async_copy(src, dst, load_sem.at[i])

    loads = [load(vec_hbm[i], vec_refs.at[i], i) for i in range(3)]
    loads += [load(xyz_hbm[i], xyz_refs.at[i], 3 + i) for i in range(3)]
    loads += [load(far_hbm, out_ref, 6)]
    for i in (4, 1, 3, 0, 5, 2, 6):
        loads[i].start()

    def list_leaf(c, total):
        def add(m, t):
            pair_list[0, t] = c
            pair_list[1, t] = ids_ref[m, c] - offset
            return t + 1

        return lax.fori_loop(0, count_ref[c], add, total)

    total = lax.fori_loop(0, leaf_dev, list_leaf, 0)
    for i in range(UNROLL + 1):
        pair_list[0, total + i] = 0
        pair_list[1, total + i] = 3 * leaf_dev
    pair_vecs[3 * leaf_dev] = jnp.zeros((2 * vec_count, leaf), BF16)

    row_ids = lax.broadcasted_iota(jnp.int32, (8, leaf), 0)

    def build(part, c):
        cols = pl.ds(pl.multiple_of(c * leaf, leaf), leaf)
        xyz = (xyz_refs[part, :, cols] - 0.5) * gain
        norm = jnp.sum(xyz * xyz, axis=0, keepdims=True)
        wide = jnp.concatenate([xyz, jnp.zeros((5, leaf), F32)], axis=0)
        theirs = jnp.where(row_ids == 3, norm, jnp.where(row_ids == 4, 1.0, wide))
        b1, b2, b3 = pieces(theirs, 3)
        slot = part * leaf_dev + c
        pair_feat[slot] = jnp.concatenate([b1, b2, b1, b2, b3, b1], axis=0).astype(BF16)
        hi, lo = pieces(vec_refs[part, :, cols] * vec_gain, 2)
        pair_vecs[slot] = jnp.concatenate([hi, lo], axis=0).astype(BF16)
        if part == 1:
            mine = jnp.where(
                row_ids == 4, norm + jitter, jnp.where(row_ids == 3, 1.0, -2.0 * wide)
            )
            a1, a2, a3 = pieces(mine, 3)
            stacked = jnp.concatenate([a1, a1, a2, a2, a1, a3], axis=0)
            own_feat[c] = stacked.astype(BF16)

    for part in (1, 0, 2):
        loads[3 + part].wait()
        loads[part].wait()
        pl.loop(0, leaf_dev, unroll=4)(lambda c, part=part: build(part, c))
    pair_feat[3 * leaf_dev] = pair_feat[leaf_dev]

    loads[6].wait()

    def squares(t):
        mine, theirs = own_feat[pair_list[0, t]], pair_feat[pair_list[1, t]]
        return lax.dot_general(
            theirs, mine, (((0,), (0,)), ((), ())), preferred_element_type=F32
        )

    def summed(t, square):
        dist = square * lax.rsqrt(square)
        matern = (LOG2E + dist) * jnp.exp2(-dist)
        high = matern.astype(BF16)
        low = (matern - high.astype(F32)).astype(BF16)
        vecs = pair_vecs[pair_list[1, t]]
        both = lax.dot_general(
            jnp.concatenate([vecs, vecs], axis=1),
            jnp.concatenate([high, low], axis=0),
            (((1,), (0,)), ((), ())),
            preferred_element_type=F32,
        )
        return both[:vec_count] + both[vec_count:]

    ahead[...] = squares(0)

    @pl.loop(0, (total + UNROLL - 1) // UNROLL)
    def _(step):
        square = ahead[...]
        done = []
        for i in range(UNROLL):
            t = step * UNROLL + i
            following = squares(t + 1)
            done.append(summed(t, square))
            square = following
        ahead[...] = square
        for i, added in enumerate(done):
            c = pair_list[0, step * UNROLL + i]
            cols = pl.ds(pl.multiple_of(c * leaf, leaf), leaf)
            out_ref[:, cols] += added


def near_call(near_list, near_count, vecs, xyz, far):
    near, leaf_dev = near_list.shape
    vec_count, width = far.shape
    leaf = width // leaf_dev

    def body(ids, count, v0, v1, v2, c0, c1, c2, far_ref, out_ref, *scratch):
        near_kernel(
            leaf_dev, ids, count, (v0, v1, v2), (c0, c1, c2), far_ref, out_ref, *scratch
        )

    vmem = pl.BlockSpec(memory_space=pltpu.VMEM)
    smem = pl.BlockSpec(memory_space=pltpu.SMEM)
    return pl.pallas_call(
        body,
        out_shape=jax.ShapeDtypeStruct((vec_count, width), F32),
        in_specs=[smem, smem] + [pl.BlockSpec(memory_space=pl.ANY)] * 7,
        out_specs=vmem,
        scratch_shapes=[
            pltpu.VMEM((leaf_dev, 48, leaf), BF16),
            pltpu.VMEM((3 * leaf_dev + 1, 48, leaf), BF16),
            pltpu.VMEM((3 * leaf_dev + 1, 2 * vec_count, leaf), BF16),
            pltpu.SMEM((2, leaf_dev * near + UNROLL + 1), jnp.int32),
            pltpu.VMEM((3, vec_count, width), F32),
            pltpu.VMEM((3, 3, width), F32),
            pltpu.SemaphoreType.DMA((7,)),
            pltpu.VMEM((leaf, leaf), F32),
        ],
        compiler_params=pltpu.CompilerParams(vmem_limit_bytes=60 * 1024 * 1024),
        cost_estimate=pl.CostEstimate(
            flops=2 * leaf_dev * near * leaf * leaf * 64,
            bytes_accessed=7 * 4 * vec_count * width,
            transcendentals=2 * leaf_dev * near * leaf * leaf,
        ),
        name="near_pairs",
    )(near_list, near_count, *vecs, *xyz, far)


def split_rows(value):
    return jnp.concatenate(pieces(value, 2), axis=0).astype(BF16)


def join_rows(value):
    half = value.shape[0] // 2
    return value[:half] + value[half:]


def dot_nn(left, right):
    return jnp.dot(left, right, preferred_element_type=F32)


def dot_nt(left, right):
    return lax.dot_general(left, right, (((1,), (1,)), ((), ())), preferred_element_type=F32)


def far_kernel(
    n_row,
    n_col,
    vec_ref,
    xyz_ref,
    basis_ref,
    transfer_hbm,
    coupling_hbm,
    list_ref,
    top_transfer_hbm,
    top_coupling_hbm,
    top_list_ref,
    far_ref,
    vec_prev,
    vec_next,
    xyz_prev,
    xyz_next,
    transfer_ref,
    coupling_ref,
    top_transfer_ref,
    top_coupling_ref,
    mats,
    couples,
    top_mats,
    top_couples,
    skel_own,
    skel_near,
    left_table,
    right_table,
    gathered,
    upper,
    field,
    near_send,
    near_recv,
    row_send,
    row_recv,
    col_send,
    col_recv,
    load_sem,
):
    n = n_row * n_col
    row, col = lax.axis_index("row"), lax.axis_index("col")
    me = row * n_col + col
    leaf_dev, rank, leaf = basis_ref.shape
    vec_count = vec_ref.shape[0]
    subtree = 2 * leaf_dev
    far_count = coupling_ref.shape[0]
    mat_rows, couple_rows = rank + 1, far_count * rank + 1
    top_count = top_coupling_ref.shape[1]
    lanes = 2 * rank
    chunks = transfer_ref.shape[1] // lanes
    has_prev, has_next = me > 0, me < n - 1
    prev_id = ((me + n - 1) % n // n_col, (me + n - 1) % n % n_col)
    next_id = ((me + 1) % n // n_col, (me + 1) % n % n_col)
    in_left = lax.broadcasted_iota(jnp.int32, (vec_count, lanes), 1) < rank

    def pick(even, odd):
        return jnp.where(in_left[: even.shape[0]], even, odd)

    loads = [
        pltpu.make_async_copy(src, dst, load_sem.at[i])
        for i, (src, dst) in enumerate(
            [
                (transfer_hbm, transfer_ref),
                (top_transfer_hbm, top_transfer_ref),
                (top_coupling_hbm, top_coupling_ref),
                (coupling_hbm, coupling_ref),
            ]
        )
    ]
    for load in loads:
        load.start()

    barrier = pltpu.get_barrier_semaphore()
    for i in range(1, n_col):
        pl.semaphore_signal(
            barrier, inc=1, device_id=(row, (col + i) % n_col), device_id_type=MESH
        )
    for i in range(1, n_row):
        pl.semaphore_signal(
            barrier, inc=1, device_id=((row + i) % n_row, col), device_id_type=MESH
        )
    from_prev_row = jnp.logical_and(col == 0, has_prev)
    from_next_row = jnp.logical_and(col == n_col - 1, has_next)

    @pl.when(from_prev_row)
    def _():
        pl.semaphore_signal(barrier, inc=1, device_id=prev_id, device_id_type=MESH)

    @pl.when(from_next_row)
    def _():
        pl.semaphore_signal(barrier, inc=1, device_id=next_id, device_id_type=MESH)

    across = jnp.logical_or(from_prev_row, from_next_row)
    peers = n_col - 1 + n_row - 1

    @pl.when(across)
    def _():
        pl.semaphore_wait(barrier, peers + 1)

    @pl.when(jnp.logical_not(across))
    def _():
        pl.semaphore_wait(barrier, peers)

    def remote(src, dst, send, recv, target):
        return pltpu.make_async_remote_copy(
            src_ref=src,
            dst_ref=dst,
            send_sem=send,
            recv_sem=recv,
            device_id=target,
            device_id_type=MESH,
        )

    top_half, low_half = pl.ds(0, vec_count // 2), pl.ds(vec_count // 2, vec_count // 2)

    def sent(vec_dst, xyz_dst, skel_dst, base, target):
        ends = [
            (vec_ref.at[top_half], vec_dst.at[top_half]),
            (vec_ref.at[low_half], vec_dst.at[low_half]),
            (xyz_ref, xyz_dst),
            (skel_own, skel_dst),
        ]
        return [
            remote(src, dst, near_send.at[base + i], near_recv.at[base + i], target)
            for i, (src, dst) in enumerate(ends)
        ]

    up = sent(vec_prev, xyz_prev, skel_near.at[0], 0, next_id)
    down = sent(vec_next, xyz_next, skel_near.at[1], 4, prev_id)

    def start_near(which):
        @pl.when(has_next)
        def _():
            for i in which:
                up[i].start()

        @pl.when(has_prev)
        def _():
            for i in which:
                down[i].start()

    def wait_near(which, sends):
        @pl.when(has_next)
        def _():
            for i in which:
                if sends:
                    up[i].wait_send()
                else:
                    down[i].wait_recv()

        @pl.when(has_prev)
        def _():
            for i in which:
                if sends:
                    down[i].wait_send()
                else:
                    up[i].wait_recv()

    start_near((0,))

    def unpack(chunk, dest, start, size, stride):
        chunk = chunk.astype(F32)
        turned = pltpu.roll(chunk, rank, 1)
        low = lax.broadcasted_iota(jnp.int32, chunk.shape, 1) < rank
        dest[pl.ds(start, size, stride=stride), :] = jnp.where(low, chunk, turned)
        dest[pl.ds(start + 1, size, stride=stride), :] = jnp.where(low, turned, chunk)

    def unpack_slots(source, dest):
        slots = source.shape[0]

        @pl.loop(0, slots // 16)
        def _(block):
            rows = pl.ds(pl.multiple_of(block * 16, 16), 16)
            for k in range(chunks):
                chunk = source[rows, k * lanes : (k + 1) * lanes]
                unpack(chunk, dest, block * 16 * mat_rows + 2 * k, 16, mat_rows)

    loads[0].wait()
    unpack_slots(transfer_ref, mats)

    def pair_mats(table, h):
        even = table[pl.ds(2 * h * mat_rows, rank), :]
        odd = table[pl.ds((2 * h + 1) * mat_rows, rank), :]
        return jnp.concatenate([even, odd], axis=0).astype(BF16)

    def leaf_pair(h):
        return basis_ref[pl.ds(2 * h, 2)].reshape(lanes, leaf)

    @pl.loop(0, leaf_dev // 2, unroll=4)
    def _(i):
        cols = pl.ds(pl.multiple_of(2 * i * leaf, 2 * leaf), 2 * leaf)
        vecs = vec_ref[:, cols]
        parts = jnp.concatenate([split_rows(vecs[:, :leaf]), split_rows(vecs[:, leaf:])], axis=0)
        both = dot_nt(parts, leaf_pair(i))
        even, odd = both[: 2 * vec_count], both[2 * vec_count :]
        skel_own[leaf_dev // 2 + i] = pick(join_rows(even), join_rows(odd))

    def two_products(one, two, left, right):
        both = dot_nn(jnp.concatenate([one, two], axis=0), jnp.concatenate([left, right], axis=1))
        rows = one.shape[0]
        return join_rows(both[:rows, :lanes]), join_rows(both[rows:, lanes:])

    half = leaf_dev // 4
    while half >= 1:
        for h in range(half, 2 * half):
            skel_own[h] = pick(
                *two_products(
                    split_rows(skel_own[2 * h]),
                    split_rows(skel_own[2 * h + 1]),
                    pair_mats(mats, 2 * h),
                    pair_mats(mats, 2 * h + 1),
                )
            )
        half //= 2
    skel_own[0] = jnp.zeros((vec_count, lanes), F32)
    gathered[me] = join_rows(dot_nn(split_rows(skel_own[1]), pair_mats(mats, 1)))

    first = [
        remote(
            gathered.at[me], gathered.at[me], row_send.at[i], row_recv.at[i], (row, (col + i) % n_col)
        )
        for i in range(1, n_col)
    ]
    for copy in first:
        copy.start()
    start_near((3,))

    for load in loads[1:]:
        load.wait()
    unpack_slots(top_transfer_ref, top_mats)
    for i in range(1, n_col):
        source = (col + n_col - i) % n_col
        remote(
            gathered.at[me],
            gathered.at[row * n_col + source],
            row_send.at[i],
            row_recv.at[i],
            (row, source),
        ).wait_recv()
    own_row = gathered.at[pl.ds(row * n_col, n_col)]
    second = [
        remote(own_row, own_row, col_send.at[i], col_recv.at[i], ((row + i) % n_row, col))
        for i in range(1, n_row)
    ]
    for copy in second:
        copy.start()
    levels = n.bit_length() - 1
    for level in range(levels):
        slot = (n + me) // (1 << (levels - 1 - level))
        for k in range(chunks):
            chunk = top_coupling_ref[slot, :, k * lanes : (k + 1) * lanes]
            unpack(chunk, top_couples, level * top_count * rank + 2 * k, top_count, rank)

    @pl.loop(0, subtree // 16 * far_count)
    def _(step):
        block, m = step // far_count, step % far_count
        rows = pl.ds(pl.multiple_of(block * 16, 16), 16)
        for k in range(chunks):
            chunk = coupling_ref[m, rows, k * lanes : (k + 1) * lanes]
            start = block * 16 * couple_rows + m * rank + 2 * k
            unpack(chunk, couples, start, 16, couple_rows)

    def fill_tables(part, pairs):
        @pl.loop(1, leaf_dev, unroll=2)
        def _(h):
            pair = pairs[h]
            turned = pltpu.roll(pair, rank, 1)
            slot = part * subtree + 2 * h
            none = jnp.zeros_like(pair)
            left_table[slot] = split_rows(pick(pair, none))
            right_table[slot] = split_rows(pick(none, turned))
            left_table[slot + 1] = split_rows(pick(turned, none))
            right_table[slot + 1] = split_rows(pick(none, pair))

    fill_tables(1, skel_own)

    for i in range(1, n_row):
        source = (row + n_row - i) % n_row
        remote(
            own_row,
            gathered.at[pl.ds(source * n_col, n_col)],
            col_send.at[i],
            col_recv.at[i],
            (source, col),
        ).wait_recv()

    start_near((1, 2))

    for d in range(n):
        upper[n + d] = gathered[d]
    half = n // 2
    while half >= 2:

        @pl.loop(half // 2, half, unroll=1 if half == 2 else 2)
        def _(g):
            h = 2 * g
            one = split_rows(pick(upper[2 * h], upper[2 * h + 1]))
            two = split_rows(pick(upper[2 * h + 2], upper[2 * h + 3]))
            upper[h], upper[h + 1] = two_products(
                one, two, pair_mats(top_mats, h), pair_mats(top_mats, h + 1)
            )

        half //= 2
    path = jnp.zeros((vec_count, lanes), F32)
    for level in range(levels):
        slot = (n + me) // (1 << (levels - 1 - level))
        partners = [upper[top_list_ref[k, slot]] for k in range(top_count)]
        own = jnp.zeros((vec_count, lanes), F32)
        for k in range(0, top_count, 2):
            block = top_couples[pl.ds((level * top_count + k) * rank, lanes), :].astype(BF16)
            own += join_rows(dot_nn(split_rows(pick(partners[k], partners[k + 1])), block))
        block = top_mats[pl.ds(slot * mat_rows, rank), :].astype(BF16)
        block = jnp.concatenate([block, block], axis=0)
        parent = split_rows(pick(path, jnp.zeros_like(path)))
        path = own + join_rows(dot_nt(parent, block))

    wait_near((3,), False)

    @pl.when(has_prev)
    def _():
        fill_tables(0, skel_near.at[0])

    @pl.when(has_next)
    def _():
        fill_tables(2, skel_near.at[1])

    offset = (me - 1) * subtree

    def coupled(j):
        sides = []
        for k in range(0, far_count, 2):
            one, two = (jnp.clip(list_ref[i, j] - offset, 0, 3 * subtree - 1) for i in (k, k + 1))
            sides.append(left_table[one] + right_table[two])
        rows = pl.ds(j * couple_rows, far_count * rank)
        return jnp.concatenate(sides, axis=1), couples[rows, :].astype(BF16)

    @pl.loop(1, leaf_dev, unroll=2)
    def _(h):
        (one, left), (two, right) = coupled(2 * h), coupled(2 * h + 1)
        field[h] = pick(*two_products(one, two, left, right))

    none = jnp.zeros((vec_count, lanes), F32)

    def masked(j):
        pair = field[j // 2]
        return split_rows(pick(pair, none) if j % 2 == 0 else pick(none, pair))

    field[1] += join_rows(dot_nt(split_rows(pick(path, none)), pair_mats(mats, 1)))
    for h in range(2, leaf_dev, 2):
        parents = jnp.concatenate([masked(h), masked(h + 1)], axis=0)
        blocks = jnp.concatenate([pair_mats(mats, h), pair_mats(mats, h + 1)], axis=0)
        both = dot_nt(parents, blocks)
        field[h] += join_rows(both[: 2 * vec_count, :lanes])
        field[h + 1] += join_rows(both[2 * vec_count :, lanes:])

    @pl.loop(0, leaf_dev // 2, unroll=4)
    def _(i):
        pair = field[leaf_dev // 2 + i]
        sides = jnp.concatenate(
            [split_rows(pick(pair, none)), split_rows(pick(none, pair))], axis=0
        )
        both = dot_nn(sides, leaf_pair(i))
        even, odd = both[: 2 * vec_count], both[2 * vec_count :]
        cols = pl.ds(pl.multiple_of(2 * i * leaf, 2 * leaf), 2 * leaf)
        far_ref[:, cols] = jnp.concatenate([join_rows(even), join_rows(odd)], axis=1)

    for copy in first + second:
        copy.wait_send()
    wait_near((0, 1, 2), False)
    wait_near((0, 1, 2, 3), True)


def far_call(n_row, n_col, vectors, coords, basis, transfer, coupling, lists, tops):
    n = n_row * n_col
    leaf_dev, rank, _ = basis.shape
    vec_count, width = vectors.shape
    far_count, subtree, _ = coupling.shape
    top_count = tops[1].shape[1]
    lanes = 2 * rank
    levels = n.bit_length() - 1
    vmem = pl.BlockSpec(memory_space=pltpu.VMEM)
    smem = pl.BlockSpec(memory_space=pltpu.SMEM)
    hbm = pl.BlockSpec(memory_space=pl.ANY)
    shape = jax.ShapeDtypeStruct
    sems = pltpu.SemaphoreType.DMA

    def body(*refs):
        far_kernel(n_row, n_col, *refs)

    return pl.pallas_call(
        body,
        out_shape=[
            shape((vec_count, width), F32),
            shape((vec_count, width), F32),
            shape((vec_count, width), F32),
            shape(coords.shape, F32),
            shape(coords.shape, F32),
        ],
        in_specs=[vmem] * 3 + [hbm] * 2 + [smem] + [hbm] * 2 + [smem],
        out_specs=[vmem] + [hbm] * 4,
        scratch_shapes=[
            pltpu.VMEM(transfer.shape, BF16),
            pltpu.VMEM(coupling.shape, BF16),
            pltpu.VMEM(tops[0].shape, BF16),
            pltpu.VMEM(tops[1].shape, BF16),
            pltpu.VMEM((subtree * (rank + 1), lanes), F32),
            pltpu.VMEM((subtree * (far_count * rank + 1), lanes), F32),
            pltpu.VMEM((2 * n * (rank + 1), lanes), F32),
            pltpu.VMEM((levels * top_count * rank, lanes), F32),
            pltpu.VMEM((leaf_dev, vec_count, lanes), F32),
            pltpu.VMEM((2, leaf_dev, vec_count, lanes), F32),
            pltpu.VMEM((3 * subtree, 2 * vec_count, lanes), BF16),
            pltpu.VMEM((3 * subtree, 2 * vec_count, lanes), BF16),
            pltpu.VMEM((n, vec_count, lanes), F32),
            pltpu.VMEM((2 * n, vec_count, lanes), F32),
            pltpu.VMEM((leaf_dev, vec_count, lanes), F32),
            sems((8,)),
            sems((8,)),
            sems((n_col,)),
            sems((n_col,)),
            sems((n_row,)),
            sems((n_row,)),
            sems((4,)),
        ],
        compiler_params=pltpu.CompilerParams(
            collective_id=0, has_side_effects=True, vmem_limit_bytes=60 * 1024 * 1024
        ),
        cost_estimate=pl.CostEstimate(
            flops=2 * 200 * 32 * lanes * lanes, bytes_accessed=10 * 1024 * 1024, transcendentals=0
        ),
        name="far_field",
    )(vectors, coords, basis, transfer, coupling, lists, *tops)


def per_device(
    n_row,
    n_col,
    vectors,
    coords,
    leaf_basis,
    transfer,
    coupling,
    near_list,
    near_count,
    local_list,
    top_transfer,
    top_coupling,
    top_list,
):
    far, vec_prev, vec_next, xyz_prev, xyz_next = far_call(
        n_row,
        n_col,
        vectors,
        coords,
        leaf_basis,
        transfer,
        jnp.transpose(coupling, (1, 0, 2)),
        jnp.transpose(local_list),
        (top_transfer, top_coupling, jnp.transpose(top_list)),
    )
    vecs = (vec_prev, vectors, vec_next)
    xyz = (xyz_prev, coords, xyz_next)
    return near_call(jnp.transpose(near_list), near_count, vecs, xyz, far)


def solution(mesh):
    return jax.shard_map(
        functools.partial(per_device, mesh.shape["row"], mesh.shape["col"]),
        mesh=mesh,
        in_specs=(
            P(None, ("row", "col")),
            P(None, ("row", "col")),
            P(("row", "col"), None, None),
            P(("row", "col"), None),
            P(("row", "col"), None, None),
            P(("row", "col"), None),
            P(("row", "col")),
            P(("row", "col"), None),
            P(),
            P(),
            P(),
        ),
        out_specs=P(None, ("row", "col")),
        check_vma=False,
    )
```

```python
import functools
import math

import jax
import jax.numpy as jnp
from jax import lax
from jax.experimental import pallas as pl
from jax.experimental.pallas import tpu as pltpu
from jax.sharding import PartitionSpec as P

ROOT_THREE = 1.7320508075688772
LENGTH_SCALE = 0.2
JITTER_SQ = 0.0001
LOG2E = 1.4426950408889634
MESH = pl.DeviceIdType.MESH
UNROLL = 4
F32 = jnp.float32
BF16 = jnp.bfloat16


def pieces(value, count):
    parts = []
    for _ in range(count):
        part = value.astype(BF16).astype(F32)
        parts.append(part)
        value = value - part
    return parts


def near_kernel(
    leaf_dev,
    ids_ref,
    count_ref,
    vec_hbm,
    xyz_hbm,
    far_hbm,
    out_ref,
    own_feat,
    pair_feat,
    pair_vecs,
    pair_list,
    vec_refs,
    xyz_refs,
    load_sem,
    ahead,
):
    vec_count, width = out_ref.shape
    leaf = width // leaf_dev
    me = lax.axis_index("row") * lax.axis_size("col") + lax.axis_index("col")
    offset = (me - 1) * leaf_dev
    gain = ROOT_THREE / LENGTH_SCALE * LOG2E
    jitter = JITTER_SQ * gain * gain
    vec_gain = 1.0 / (LOG2E * math.sqrt(leaf))

    def load(src, dst, i):
        return pltpu.make_async_copy(src, dst, load_sem.at[i])

    loads = [load(vec_hbm[i], vec_refs.at[i], i) for i in range(3)]
    loads += [load(xyz_hbm[i], xyz_refs.at[i], 3 + i) for i in range(3)]
    loads += [load(far_hbm, out_ref, 6)]
    for i in (4, 1, 3, 0, 5, 2, 6):
        loads[i].start()

    def list_leaf(c, total):
        def add(m, t):
            pair_list[0, t] = c
            pair_list[1, t] = ids_ref[m, c] - offset
            return t + 1

        return lax.fori_loop(0, count_ref[c], add, total)

    total = lax.fori_loop(0, leaf_dev, list_leaf, 0)
    for i in range(UNROLL + 1):
        pair_list[0, total + i] = 0
        pair_list[1, total + i] = 3 * leaf_dev
    pair_vecs[3 * leaf_dev] = jnp.zeros((2 * vec_count, leaf), BF16)

    row_ids = lax.broadcasted_iota(jnp.int32, (8, leaf), 0)

    def build(part, c):
        cols = pl.ds(pl.multiple_of(c * leaf, leaf), leaf)
        xyz = (xyz_refs[part, :, cols] - 0.5) * gain
        norm = jnp.sum(xyz * xyz, axis=0, keepdims=True)
        wide = jnp.concatenate([xyz, jnp.zeros((5, leaf), F32)], axis=0)
        theirs = jnp.where(row_ids == 3, norm, jnp.where(row_ids == 4, 1.0, wide))
        b1, b2, b3 = pieces(theirs, 3)
        slot = part * leaf_dev + c
        pair_feat[slot] = jnp.concatenate([b1, b2, b1, b2, b3, b1], axis=0).astype(BF16)
        hi, lo = pieces(vec_refs[part, :, cols] * vec_gain, 2)
        pair_vecs[slot] = jnp.concatenate([hi, lo], axis=0).astype(BF16)
        if part == 1:
            mine = jnp.where(
                row_ids == 4, norm + jitter, jnp.where(row_ids == 3, 1.0, -2.0 * wide)
            )
            a1, a2, a3 = pieces(mine, 3)
            stacked = jnp.concatenate([a1, a1, a2, a2, a1, a3], axis=0)
            own_feat[c] = stacked.astype(BF16)

    for part in (1, 0, 2):
        loads[3 + part].wait()
        loads[part].wait()
        pl.loop(0, leaf_dev, unroll=4)(lambda c, part=part: build(part, c))
    pair_feat[3 * leaf_dev] = pair_feat[leaf_dev]

    loads[6].wait()

    def squares(t):
        mine, theirs = own_feat[pair_list[0, t]], pair_feat[pair_list[1, t]]
        return lax.dot_general(
            theirs, mine, (((0,), (0,)), ((), ())), preferred_element_type=F32
        )

    def summed(t, square):
        dist = square * lax.rsqrt(square)
        matern = (LOG2E + dist) * jnp.exp2(-dist)
        high = matern.astype(BF16)
        low = (matern - high.astype(F32)).astype(BF16)
        vecs = pair_vecs[pair_list[1, t]]
        both = lax.dot_general(
            jnp.concatenate([vecs, vecs], axis=1),
            jnp.concatenate([high, low], axis=0),
            (((1,), (0,)), ((), ())),
            preferred_element_type=F32,
        )
        return both[:vec_count] + both[vec_count:]

    ahead[...] = squares(0)

    @pl.loop(0, (total + UNROLL - 1) // UNROLL)
    def _(step):
        square = ahead[...]
        done = []
        for i in range(UNROLL):
            t = step * UNROLL + i
            following = squares(t + 1)
            done.append(summed(t, square))
            square = following
        ahead[...] = square
        for i, added in enumerate(done):
            c = pair_list[0, step * UNROLL + i]
            cols = pl.ds(pl.multiple_of(c * leaf, leaf), leaf)
            out_ref[:, cols] += added


def near_call(near_list, near_count, vecs, xyz, far):
    near, leaf_dev = near_list.shape
    vec_count, width = far.shape
    leaf = width // leaf_dev

    def body(ids, count, v0, v1, v2, c0, c1, c2, far_ref, out_ref, *scratch):
        near_kernel(
            leaf_dev, ids, count, (v0, v1, v2), (c0, c1, c2), far_ref, out_ref, *scratch
        )

    vmem = pl.BlockSpec(memory_space=pltpu.VMEM)
    smem = pl.BlockSpec(memory_space=pltpu.SMEM)
    return pl.pallas_call(
        body,
        out_shape=jax.ShapeDtypeStruct((vec_count, width), F32),
        in_specs=[smem, smem] + [pl.BlockSpec(memory_space=pl.ANY)] * 7,
        out_specs=vmem,
        scratch_shapes=[
            pltpu.VMEM((leaf_dev, 48, leaf), BF16),
            pltpu.VMEM((3 * leaf_dev + 1, 48, leaf), BF16),
            pltpu.VMEM((3 * leaf_dev + 1, 2 * vec_count, leaf), BF16),
            pltpu.SMEM((2, leaf_dev * near + UNROLL + 1), jnp.int32),
            pltpu.VMEM((3, vec_count, width), F32),
            pltpu.VMEM((3, 3, width), F32),
            pltpu.SemaphoreType.DMA((7,)),
            pltpu.VMEM((leaf, leaf), F32),
        ],
        compiler_params=pltpu.CompilerParams(vmem_limit_bytes=60 * 1024 * 1024),
        cost_estimate=pl.CostEstimate(
            flops=2 * leaf_dev * near * leaf * leaf * 64,
            bytes_accessed=7 * 4 * vec_count * width,
            transcendentals=2 * leaf_dev * near * leaf * leaf,
        ),
        name="near_pairs",
    )(near_list, near_count, *vecs, *xyz, far)


def split_rows(value):
    return jnp.concatenate(pieces(value, 2), axis=0).astype(BF16)


def join_rows(value):
    half = value.shape[0] // 2
    return value[:half] + value[half:]


def dot_nn(left, right):
    return jnp.dot(left, right, preferred_element_type=F32)


def dot_nt(left, right):
    return lax.dot_general(left, right, (((1,), (1,)), ((), ())), preferred_element_type=F32)


def far_kernel(
    n_row,
    n_col,
    vec_ref,
    xyz_ref,
    basis_ref,
    transfer_hbm,
    coupling_hbm,
    list_ref,
    top_transfer_hbm,
    top_coupling_hbm,
    top_list_ref,
    far_ref,
    vec_prev,
    vec_next,
    xyz_prev,
    xyz_next,
    transfer_ref,
    coupling_ref,
    top_transfer_ref,
    top_coupling_ref,
    mats,
    couples,
    top_mats,
    top_couples,
    skel_own,
    skel_near,
    left_table,
    right_table,
    gathered,
    upper,
    field,
    near_send,
    near_recv,
    row_send,
    row_recv,
    col_send,
    col_recv,
    load_sem,
):
    n = n_row * n_col
    row, col = lax.axis_index("row"), lax.axis_index("col")
    me = row * n_col + col
    leaf_dev, rank, leaf = basis_ref.shape
    vec_count = vec_ref.shape[0]
    subtree = 2 * leaf_dev
    far_count = coupling_ref.shape[0]
    mat_rows, couple_rows = rank + 1, far_count * rank + 1
    top_count = top_coupling_ref.shape[1]
    lanes = 2 * rank
    chunks = transfer_ref.shape[1] // lanes
    has_prev, has_next = me > 0, me < n - 1
    prev_id = ((me + n - 1) % n // n_col, (me + n - 1) % n % n_col)
    next_id = ((me + 1) % n // n_col, (me + 1) % n % n_col)
    in_left = lax.broadcasted_iota(jnp.int32, (vec_count, lanes), 1) < rank

    def pick(even, odd):
        return jnp.where(in_left[: even.shape[0]], even, odd)

    loads = [
        pltpu.make_async_copy(src, dst, load_sem.at[i])
        for i, (src, dst) in enumerate(
            [
                (transfer_hbm, transfer_ref),
                (top_transfer_hbm, top_transfer_ref),
                (top_coupling_hbm, top_coupling_ref),
                (coupling_hbm, coupling_ref),
            ]
        )
    ]
    for load in loads:
        load.start()

    barrier = pltpu.get_barrier_semaphore()
    for i in range(1, n_col):
        pl.semaphore_signal(
            barrier, inc=1, device_id=(row, (col + i) % n_col), device_id_type=MESH
        )
    for i in range(1, n_row):
        pl.semaphore_signal(
            barrier, inc=1, device_id=((row + i) % n_row, col), device_id_type=MESH
        )
    from_prev_row = jnp.logical_and(col == 0, has_prev)
    from_next_row = jnp.logical_and(col == n_col - 1, has_next)

    @pl.when(from_prev_row)
    def _():
        pl.semaphore_signal(barrier, inc=1, device_id=prev_id, device_id_type=MESH)

    @pl.when(from_next_row)
    def _():
        pl.semaphore_signal(barrier, inc=1, device_id=next_id, device_id_type=MESH)

    across = jnp.logical_or(from_prev_row, from_next_row)
    peers = n_col - 1 + n_row - 1

    @pl.when(across)
    def _():
        pl.semaphore_wait(barrier, peers + 1)

    @pl.when(jnp.logical_not(across))
    def _():
        pl.semaphore_wait(barrier, peers)

    def remote(src, dst, send, recv, target):
        return pltpu.make_async_remote_copy(
            src_ref=src,
            dst_ref=dst,
            send_sem=send,
            recv_sem=recv,
            device_id=target,
            device_id_type=MESH,
        )

    top_half, low_half = pl.ds(0, vec_count // 2), pl.ds(vec_count // 2, vec_count // 2)

    def sent(vec_dst, xyz_dst, skel_dst, base, target):
        ends = [
            (vec_ref.at[top_half], vec_dst.at[top_half]),
            (vec_ref.at[low_half], vec_dst.at[low_half]),
            (xyz_ref, xyz_dst),
            (skel_own, skel_dst),
        ]
        return [
            remote(src, dst, near_send.at[base + i], near_recv.at[base + i], target)
            for i, (src, dst) in enumerate(ends)
        ]

    up = sent(vec_prev, xyz_prev, skel_near.at[0], 0, next_id)
    down = sent(vec_next, xyz_next, skel_near.at[1], 4, prev_id)

    def start_near(which):
        @pl.when(has_next)
        def _():
            for i in which:
                up[i].start()

        @pl.when(has_prev)
        def _():
            for i in which:
                down[i].start()

    def wait_near(which, sends):
        @pl.when(has_next)
        def _():
            for i in which:
                if sends:
                    up[i].wait_send()
                else:
                    down[i].wait_recv()

        @pl.when(has_prev)
        def _():
            for i in which:
                if sends:
                    down[i].wait_send()
                else:
                    up[i].wait_recv()

    start_near((0,))

    def unpack(chunk, dest, start, size, stride):
        chunk = chunk.astype(F32)
        turned = pltpu.roll(chunk, rank, 1)
        low = lax.broadcasted_iota(jnp.int32, chunk.shape, 1) < rank
        dest[pl.ds(start, size, stride=stride), :] = jnp.where(low, chunk, turned)
        dest[pl.ds(start + 1, size, stride=stride), :] = jnp.where(low, turned, chunk)

    def unpack_slots(source, dest):
        slots = source.shape[0]

        @pl.loop(0, slots // 16)
        def _(block):
            rows = pl.ds(pl.multiple_of(block * 16, 16), 16)
            for k in range(chunks):
                chunk = source[rows, k * lanes : (k + 1) * lanes]
                unpack(chunk, dest, block * 16 * mat_rows + 2 * k, 16, mat_rows)

    loads[0].wait()
    unpack_slots(transfer_ref, mats)

    def pair_mats(table, h):
        even = table[pl.ds(2 * h * mat_rows, rank), :]
        odd = table[pl.ds((2 * h + 1) * mat_rows, rank), :]
        return jnp.concatenate([even, odd], axis=0).astype(BF16)

    def leaf_pair(h):
        return basis_ref[pl.ds(2 * h, 2)].reshape(lanes, leaf)

    @pl.loop(0, leaf_dev // 2, unroll=4)
    def _(i):
        cols = pl.ds(pl.multiple_of(2 * i * leaf, 2 * leaf), 2 * leaf)
        vecs = vec_ref[:, cols]
        parts = jnp.concatenate([split_rows(vecs[:, :leaf]), split_rows(vecs[:, leaf:])], axis=0)
        both = dot_nt(parts, leaf_pair(i))
        even, odd = both[: 2 * vec_count], both[2 * vec_count :]
        skel_own[leaf_dev // 2 + i] = pick(join_rows(even), join_rows(odd))

    def two_products(one, two, left, right):
        both = dot_nn(jnp.concatenate([one, two], axis=0), jnp.concatenate([left, right], axis=1))
        rows = one.shape[0]
        return join_rows(both[:rows, :lanes]), join_rows(both[rows:, lanes:])

    half = leaf_dev // 4
    while half >= 1:
        for h in range(half, 2 * half):
            skel_own[h] = pick(
                *two_products(
                    split_rows(skel_own[2 * h]),
                    split_rows(skel_own[2 * h + 1]),
                    pair_mats(mats, 2 * h),
                    pair_mats(mats, 2 * h + 1),
                )
            )
        half //= 2
    skel_own[0] = jnp.zeros((vec_count, lanes), F32)
    gathered[me] = join_rows(dot_nn(split_rows(skel_own[1]), pair_mats(mats, 1)))

    first = [
        remote(
            gathered.at[me], gathered.at[me], row_send.at[i], row_recv.at[i], (row, (col + i) % n_col)
        )
        for i in range(1, n_col)
    ]
    for copy in first:
        copy.start()
    start_near((3,))

    for load in loads[1:]:
        load.wait()
    unpack_slots(top_transfer_ref, top_mats)
    for i in range(1, n_col):
        source = (col + n_col - i) % n_col
        remote(
            gathered.at[me],
            gathered.at[row * n_col + source],
            row_send.at[i],
            row_recv.at[i],
            (row, source),
        ).wait_recv()
    own_row = gathered.at[pl.ds(row * n_col, n_col)]
    second = [
        remote(own_row, own_row, col_send.at[i], col_recv.at[i], ((row + i) % n_row, col))
        for i in range(1, n_row)
    ]
    for copy in second:
        copy.start()
    start_near((1, 2))
    levels = n.bit_length() - 1
    for level in range(levels):
        slot = (n + me) // (1 << (levels - 1 - level))
        for k in range(chunks):
            chunk = top_coupling_ref[slot, :, k * lanes : (k + 1) * lanes]
            unpack(chunk, top_couples, level * top_count * rank + 2 * k, top_count, rank)

    @pl.loop(0, subtree // 16 * far_count)
    def _(step):
        block, m = step // far_count, step % far_count
        rows = pl.ds(pl.multiple_of(block * 16, 16), 16)
        for k in range(chunks):
            chunk = coupling_ref[m, rows, k * lanes : (k + 1) * lanes]
            start = block * 16 * couple_rows + m * rank + 2 * k
            unpack(chunk, couples, start, 16, couple_rows)

    def fill_tables(part, pairs):
        @pl.loop(1, leaf_dev, unroll=2)
        def _(h):
            pair = pairs[h]
            turned = pltpu.roll(pair, rank, 1)
            slot = part * subtree + 2 * h
            none = jnp.zeros_like(pair)
            left_table[slot] = split_rows(pick(pair, none))
            right_table[slot] = split_rows(pick(none, turned))
            left_table[slot + 1] = split_rows(pick(turned, none))
            right_table[slot + 1] = split_rows(pick(none, pair))

    fill_tables(1, skel_own)

    for i in range(1, n_row):
        source = (row + n_row - i) % n_row
        remote(
            own_row,
            gathered.at[pl.ds(source * n_col, n_col)],
            col_send.at[i],
            col_recv.at[i],
            (source, col),
        ).wait_recv()

    for d in range(n):
        upper[n + d] = gathered[d]
    half = n // 2
    while half >= 2:

        @pl.loop(half // 2, half, unroll=1 if half == 2 else 2)
        def _(g):
            h = 2 * g
            one = split_rows(pick(upper[2 * h], upper[2 * h + 1]))
            two = split_rows(pick(upper[2 * h + 2], upper[2 * h + 3]))
            upper[h], upper[h + 1] = two_products(
                one, two, pair_mats(top_mats, h), pair_mats(top_mats, h + 1)
            )

        half //= 2
    path = jnp.zeros((vec_count, lanes), F32)
    for level in range(levels):
        slot = (n + me) // (1 << (levels - 1 - level))
        partners = [upper[top_list_ref[k, slot]] for k in range(top_count)]
        own = jnp.zeros((vec_count, lanes), F32)
        for k in range(0, top_count, 2):
            block = top_couples[pl.ds((level * top_count + k) * rank, lanes), :].astype(BF16)
            own += join_rows(dot_nn(split_rows(pick(partners[k], partners[k + 1])), block))
        block = top_mats[pl.ds(slot * mat_rows, rank), :].astype(BF16)
        block = jnp.concatenate([block, block], axis=0)
        parent = split_rows(pick(path, jnp.zeros_like(path)))
        path = own + join_rows(dot_nt(parent, block))

    wait_near((3,), False)

    @pl.when(has_prev)
    def _():
        fill_tables(0, skel_near.at[0])

    @pl.when(has_next)
    def _():
        fill_tables(2, skel_near.at[1])

    offset = (me - 1) * subtree

    def coupled(j):
        sides = []
        for k in range(0, far_count, 2):
            one, two = (jnp.clip(list_ref[i, j] - offset, 0, 3 * subtree - 1) for i in (k, k + 1))
            sides.append(left_table[one] + right_table[two])
        rows = pl.ds(j * couple_rows, far_count * rank)
        return jnp.concatenate(sides, axis=1), couples[rows, :].astype(BF16)

    @pl.loop(1, leaf_dev, unroll=2)
    def _(h):
        (one, left), (two, right) = coupled(2 * h), coupled(2 * h + 1)
        field[h] = pick(*two_products(one, two, left, right))

    none = jnp.zeros((vec_count, lanes), F32)

    def masked(j):
        pair = field[j // 2]
        return split_rows(pick(pair, none) if j % 2 == 0 else pick(none, pair))

    field[1] += join_rows(dot_nt(split_rows(pick(path, none)), pair_mats(mats, 1)))
    for h in range(2, leaf_dev, 2):
        parents = jnp.concatenate([masked(h), masked(h + 1)], axis=0)
        blocks = jnp.concatenate([pair_mats(mats, h), pair_mats(mats, h + 1)], axis=0)
        both = dot_nt(parents, blocks)
        field[h] += join_rows(both[: 2 * vec_count, :lanes])
        field[h + 1] += join_rows(both[2 * vec_count :, lanes:])

    @pl.loop(0, leaf_dev // 2, unroll=4)
    def _(i):
        pair = field[leaf_dev // 2 + i]
        sides = jnp.concatenate(
            [split_rows(pick(pair, none)), split_rows(pick(none, pair))], axis=0
        )
        both = dot_nn(sides, leaf_pair(i))
        even, odd = both[: 2 * vec_count], both[2 * vec_count :]
        cols = pl.ds(pl.multiple_of(2 * i * leaf, 2 * leaf), 2 * leaf)
        far_ref[:, cols] = jnp.concatenate([join_rows(even), join_rows(odd)], axis=1)

    for copy in first + second:
        copy.wait_send()
    wait_near((0, 1, 2), False)
    wait_near((0, 1, 2, 3), True)


def far_call(n_row, n_col, vectors, coords, basis, transfer, coupling, lists, tops):
    n = n_row * n_col
    leaf_dev, rank, _ = basis.shape
    vec_count, width = vectors.shape
    far_count, subtree, _ = coupling.shape
    top_count = tops[1].shape[1]
    lanes = 2 * rank
    levels = n.bit_length() - 1
    vmem = pl.BlockSpec(memory_space=pltpu.VMEM)
    smem = pl.BlockSpec(memory_space=pltpu.SMEM)
    hbm = pl.BlockSpec(memory_space=pl.ANY)
    shape = jax.ShapeDtypeStruct
    sems = pltpu.SemaphoreType.DMA

    def body(*refs):
        far_kernel(n_row, n_col, *refs)

    return pl.pallas_call(
        body,
        out_shape=[
            shape((vec_count, width), F32),
            shape((vec_count, width), F32),
            shape((vec_count, width), F32),
            shape(coords.shape, F32),
            shape(coords.shape, F32),
        ],
        in_specs=[vmem] * 3 + [hbm] * 2 + [smem] + [hbm] * 2 + [smem],
        out_specs=[vmem] + [hbm] * 4,
        scratch_shapes=[
            pltpu.VMEM(transfer.shape, BF16),
            pltpu.VMEM(coupling.shape, BF16),
            pltpu.VMEM(tops[0].shape, BF16),
            pltpu.VMEM(tops[1].shape, BF16),
            pltpu.VMEM((subtree * (rank + 1), lanes), F32),
            pltpu.VMEM((subtree * (far_count * rank + 1), lanes), F32),
            pltpu.VMEM((2 * n * (rank + 1), lanes), F32),
            pltpu.VMEM((levels * top_count * rank, lanes), F32),
            pltpu.VMEM((leaf_dev, vec_count, lanes), F32),
            pltpu.VMEM((2, leaf_dev, vec_count, lanes), F32),
            pltpu.VMEM((3 * subtree, 2 * vec_count, lanes), BF16),
            pltpu.VMEM((3 * subtree, 2 * vec_count, lanes), BF16),
            pltpu.VMEM((n, vec_count, lanes), F32),
            pltpu.VMEM((2 * n, vec_count, lanes), F32),
            pltpu.VMEM((leaf_dev, vec_count, lanes), F32),
            sems((8,)),
            sems((8,)),
            sems((n_col,)),
            sems((n_col,)),
            sems((n_row,)),
            sems((n_row,)),
            sems((4,)),
        ],
        compiler_params=pltpu.CompilerParams(
            collective_id=0, has_side_effects=True, vmem_limit_bytes=60 * 1024 * 1024
        ),
        cost_estimate=pl.CostEstimate(
            flops=2 * 200 * 32 * lanes * lanes, bytes_accessed=10 * 1024 * 1024, transcendentals=0
        ),
        name="far_field",
    )(vectors, coords, basis, transfer, coupling, lists, *tops)


def per_device(
    n_row,
    n_col,
    vectors,
    coords,
    leaf_basis,
    transfer,
    coupling,
    near_list,
    near_count,
    local_list,
    top_transfer,
    top_coupling,
    top_list,
):
    far, vec_prev, vec_next, xyz_prev, xyz_next = far_call(
        n_row,
        n_col,
        vectors,
        coords,
        leaf_basis,
        transfer,
        jnp.transpose(coupling, (1, 0, 2)),
        jnp.transpose(local_list),
        (top_transfer, top_coupling, jnp.transpose(top_list)),
    )
    vecs = (vec_prev, vectors, vec_next)
    xyz = (xyz_prev, coords, xyz_next)
    return near_call(jnp.transpose(near_list), near_count, vecs, xyz, far)


def solution(mesh):
    return jax.shard_map(
        functools.partial(per_device, mesh.shape["row"], mesh.shape["col"]),
        mesh=mesh,
        in_specs=(
            P(None, ("row", "col")),
            P(None, ("row", "col")),
            P(("row", "col"), None, None),
            P(("row", "col"), None),
            P(("row", "col"), None, None),
            P(("row", "col"), None),
            P(("row", "col")),
            P(("row", "col"), None),
            P(),
            P(),
            P(),
        ),
        out_specs=P(None, ("row", "col")),
        check_vma=False,
    )
```
